256 devices in a mesh: dp: 8 (over y, core), expert: 32 (over z, x).
Axes of the slice: x: 4, y: 4, z: 8, core: 2. Of those that a mesh axis runs over, the one named last changes fastest.
Arguments:
- frames_in: bfloat16 [256, 256, 1024], P(('dp', 'expert')), may hold values from -6 to 6
- pit_order: int32 [128, 2], replicated, may hold values from 0 to 1, each once within a row
- expert_ids: int32 [256, 256, 2], P(('dp', 'expert')), may hold values from 0 to 31, all different within a row; in each aligned block of 256 rows (0 to 255, 256 to 511, ..., all dimensions but the last counted through in order) at most 20 rows name the same one
- norm_gains: float32 [2, 1024], replicated, may hold values from 0.25 to 1.75
- attn_qkv: bfloat16 [3, 1024, 1024], P(None, 'expert'), may hold values from -6 to 6
- attn_out: bfloat16 [1024, 1024], P('expert'), may hold values from -0.1875 to 0.1875
- router: float32 [1024, 32], replicated, may hold values from -0.046875 to 0.046875
- expert_in: bfloat16 [32, 1024, 4096], P('expert', None, 'dp'), may hold values from -0.1875 to 0.1875
- expert_out: bfloat16 [32, 4096, 1024], P('expert', 'dp'), may hold values from -0.09375 to 0.09375
Outputs:
- layer_out: bfloat16 [256, 256, 1024], P(('dp', 'expert'))
The draws below stay inside these ranges and needn't reach their ends.
Inputs may be any that keep to these rules, and one draw needn't show every extreme that they name: `expert_ids`: at most 20 frames of one stream name the same expert, and in every draw some stream names some expert exactly 20 times; each frame names 2 different experts.
All inputs are finite; a program needn't handle non-finite values.
Results may differ from the reference program's by a relative error of at most 0.011.
Values may be sent and summed in bfloat16 or wider, within the bound.
A program may use at most 128 MiB of HBM per device.

```python
import math
import jax
import jax.numpy as jnp
import numpy as np
from jax import lax

D = 1024
FF = 4096
HEADS = 16
HEAD_DIM = 64
TOP = 2
FRAMES = 256
EXPERTS = 32
CAP = 20
STREAMS = 256
MEETINGS = 128
N_DP = 8


def draw_attn_qkv(key, part):
    base = jnp.clip(jax.random.normal(key, (3, D, D), jnp.float32), -6.0, 6.0) * D ** (-0.5)
    return jnp.clip(base, -6.0, 6.0).astype(jnp.bfloat16)


def shard_levels(own_key, extent, split, smallest, top_value):
    level, own = 1.0, jax.random.fold_in(own_key, 6)
    for axis_at, blocks in split:
        draws = jnp.exp(jax.random.uniform(jax.random.fold_in(own, axis_at), (blocks,), jnp.float32, smallest / len(split), top_value / len(split)))
        level = level * jnp.repeat(draws, extent[axis_at] // blocks).reshape([-1 if axis == axis_at else 1 for axis in range(len(extent))])
    return level


def shared_out(rng, own, number, rows, amount, top, most, skew):
    ranking = jax.random.permutation(rng, amount)
    crowded, common = portions_of(amount, rows * top, most, skew, True), portions_of(amount, rows * top, most, skew, False)
    places = jnp.arange(amount)

    def named(sizes, turn):
        used = int((sizes > 0).sum())
        fixed = max(1, used // 4)
        shifted = fixed + (places - fixed + turn * (used - fixed)) % max(1, amount - fixed)
        return jnp.zeros((amount,), jnp.int32).at[ranking[jnp.where(places < fixed, places, shifted)]].set(jnp.asarray(sizes, jnp.int32))

    sizes = jnp.where(number % 4 == 0, named(crowded, number // 4), named(common, number - number // 4 - 1))
    mixed = jax.random.permutation(jax.random.fold_in(own, 3), amount)
    source_of, taker = mixed[0:amount // 2 * 2:2], mixed[1:amount // 2 * 2:2]
    slack = jnp.minimum(sizes[source_of] - 1, most - sizes[taker]) // 2
    slack = jnp.where((source_of == ranking[0]) | (taker == ranking[0]) | (sizes[taker] == 0), 0, jnp.maximum(slack, 0))
    shifted = jax.random.randint(jax.random.fold_in(own, 4), (amount // 2,), 0, 1 << 20) % (slack + 1)
    sizes = sizes.at[source_of].add(-shifted).at[taker].add(shifted)
    labels = jnp.searchsorted(jnp.cumsum(sizes), jnp.arange(rows * top), side="right").astype(jnp.int32)
    table = labels.reshape(top, rows).T
    table = table[jax.random.permutation(jax.random.fold_in(own, 1), rows)]
    turn = jax.random.randint(jax.random.fold_in(own, 2), (rows, 1), 0, top)
    return jnp.take_along_axis(table, (jnp.arange(top)[None, :] + turn) % top, axis=1)


def portions_of(count, total, limit, lean, full):
    weights = [(1 << 20) // math.isqrt(standing ** lean) + 1 for standing in range(1, count + 1)]
    largest = limit if full else min(limit, max(-(-total // count), total * weights[0] // sum(weights)))
    least = 1 if total - largest >= count - 1 else 0
    counts, spare = [largest] + [least] * (count - 1), total - largest - least * (count - 1)
    while spare > 0:
        movable = [i for i in range(1, count) if counts[i] < largest] or [i for i in range(1, count) if counts[i] < limit]
        whole, budget = sum([weights[i] for i in movable]), spare
        for i in movable:
            extra = min(limit - counts[i], max(1, budget * weights[i] // whole), spare)
            counts[i] = counts[i] + extra
            spare = spare - extra
    return np.array(counts)


def scatter_about(stream_key, dims, scale, bound, cuts=(), kind=jnp.bfloat16):
    values = jax.random.normal(stream_key, dims, jnp.float32) * scale
    if len(cuts) > 0:
        values = shard_levels(stream_key, dims, cuts, -0.22, 0.18) * values
    return jnp.clip(values, min=-bound, max=bound).astype(kind)


def setup_inputs(seed: int = 0) -> dict:
    key_list = jax.random.split(jax.random.key(seed), 10)
    frames_in = scatter_about(key_list[0], (STREAMS, FRAMES, D), 1.0, 6.0, ((0, 256),))
    pit_order = jax.vmap(lambda own: jax.random.permutation(own, 2))(jax.random.split(key_list[1], MEETINGS)).reshape((MEETINGS, 2)).astype(jnp.int32)
    expert_ids_keys = jax.random.split(jax.random.fold_in(key_list[2], 1), STREAMS * FRAMES // FRAMES)
    expert_ids_turns = jax.random.permutation(jax.random.fold_in(key_list[2], 3), STREAMS * FRAMES // FRAMES)
    expert_ids = jax.vmap(lambda own, number: shared_out(jax.random.fold_in(key_list[2], 2), own, number, FRAMES, EXPERTS, TOP, CAP, 2))(expert_ids_keys, expert_ids_turns).reshape((STREAMS, FRAMES, TOP))
    norm_gains = jnp.clip(1.0 + 0.15 * jax.random.normal(key_list[3], (2, D), jnp.float32), 0.25, 1.75)
    attn_qkv = draw_attn_qkv(jax.random.fold_in(key_list[9], 71), 0)
    attn_out = scatter_about(key_list[5], (D, D), D ** -0.5, 0.1875, ((0, 32),))
    router = scatter_about(key_list[6], (D, EXPERTS), (16 * D) ** -0.5, 0.046875, (), jnp.float32)
    expert_in = scatter_about(key_list[7], (EXPERTS, D, FF), D ** -0.5, 0.1875, ((0, 32), (2, 8)))
    expert_out = scatter_about(key_list[8], (EXPERTS, FF, D), FF ** -0.5, 0.09375, ((0, 32), (1, 8)))
    return {"frames_in": frames_in, "pit_order": pit_order, "expert_ids": expert_ids, "norm_gains": norm_gains, "attn_qkv": attn_qkv, "attn_out": attn_out, "router": router, "expert_in": expert_in, "expert_out": expert_out}


epsilon = 1e-05

def layer_norm(values, gain):
    mean = lax.optimization_barrier(jnp.mean(values, axis=-1, keepdims=True))
    centred = values - mean
    spread = lax.optimization_barrier(jnp.mean(centred * centred, axis=-1, keepdims=True))
    return centred * lax.rsqrt(spread + epsilon) * gain

def attend(stream, norm_gains, attn_qkv, attn_out):
    resid = stream.astype(jnp.float32)
    normed = layer_norm(resid, norm_gains[0]).astype(jnp.bfloat16)
    query = jnp.dot(normed, attn_qkv[0], preferred_element_type=jnp.float32).astype(jnp.bfloat16)
    keys = jnp.dot(normed, attn_qkv[1], preferred_element_type=jnp.float32).astype(jnp.bfloat16)
    values = jnp.dot(normed, attn_qkv[2], preferred_element_type=jnp.float32).astype(jnp.bfloat16)
    query = query.reshape(FRAMES, HEADS, HEAD_DIM).astype(jnp.float32)
    keys = keys.reshape(FRAMES, HEADS, HEAD_DIM).astype(jnp.float32)
    values = values.reshape(FRAMES, HEADS, HEAD_DIM).astype(jnp.float32)
    scores = jnp.einsum('qhd,khd->hqk', query, keys) / HEAD_DIM ** 0.5
    top = lax.optimization_barrier(jnp.max(scores, axis=-1, keepdims=True))
    weights = jnp.exp(scores - top)
    probs = (weights / lax.optimization_barrier(jnp.sum(weights, axis=-1, keepdims=True))).astype(jnp.bfloat16)
    context = jnp.einsum('hqk,khd->qhd', probs.astype(jnp.float32), values)
    context = context.reshape(FRAMES, D).astype(jnp.bfloat16)
    attended = jnp.dot(context, attn_out, preferred_element_type=jnp.float32)
    mixed = (resid + attended).astype(jnp.bfloat16)
    normed2 = layer_norm(mixed.astype(jnp.float32), norm_gains[1]).astype(jnp.bfloat16)
    return (mixed, normed2)

def slot_positions(ids):
    flat = ids.reshape(-1).astype(jnp.int32)
    onehot = (flat[:, None] == jnp.arange(EXPERTS, dtype=jnp.int32)[None, :]).astype(jnp.int32)
    ranks = lax.optimization_barrier(jnp.sum(onehot * (jnp.cumsum(onehot, axis=0) - 1), axis=1)).astype(jnp.int32)
    return (flat * CAP + ranks).astype(jnp.int32)

def fill_slots(rows, positions):
    return jnp.zeros((EXPERTS * CAP, D), jnp.bfloat16).at[positions].set(rows)

def run_expert(inputs):
    rows, first, second = inputs
    hidden = jax.nn.silu(jnp.dot(rows, first, preferred_element_type=jnp.float32)).astype(jnp.bfloat16)
    width = FF // N_DP
    total = jnp.zeros((rows.shape[0], D), jnp.float32)
    for index in range(N_DP):
        part = jnp.dot(hidden[:, index * width:(index + 1) * width], second[index * width:(index + 1) * width], preferred_element_type=jnp.float32).astype(jnp.bfloat16)
        part = lax.optimization_barrier(part)
        total = total + part.astype(jnp.float32)
    return total.astype(jnp.bfloat16)

def reference(frames_in, pit_order, expert_ids, norm_gains, attn_qkv, attn_out, router, expert_in, expert_out):
    pairs = frames_in.reshape(2, MEETINGS, FRAMES, D)
    first = jnp.where((pit_order[:, 0] == 0)[:, None, None], pairs[0], pairs[1])
    second = jnp.where((pit_order[:, 1] == 0)[:, None, None], pairs[0], pairs[1])
    streams = jnp.concatenate([first, second], axis=0)
    mixed, normed2 = lax.map(lambda one: attend(one, norm_gains, attn_qkv, attn_out), streams)
    logits = jnp.dot(normed2.reshape(STREAMS * FRAMES, D).astype(jnp.float32), router, precision=lax.Precision.HIGHEST)
    logits = logits.reshape(STREAMS, FRAMES, EXPERTS)
    picked = jnp.take_along_axis(logits, expert_ids, axis=2)
    gate0 = jax.nn.sigmoid(picked[:, :, 0] - picked[:, :, 1])
    gate1 = 1.0 - gate0
    positions = jax.vmap(slot_positions)(expert_ids)
    rows = jnp.repeat(normed2, TOP, axis=1)
    slots = jax.vmap(fill_slots)(rows, positions)
    slots = slots.reshape(STREAMS, EXPERTS, CAP, D).transpose(1, 0, 2, 3).reshape(EXPERTS, STREAMS * CAP, D)
    answer = lax.map(run_expert, (slots, expert_in, expert_out))
    answer = answer.reshape(EXPERTS, STREAMS, CAP, D).transpose(1, 0, 2, 3).reshape(STREAMS, EXPERTS * CAP, D)
    back = jax.vmap(lambda table, where: table[where])(answer, positions)
    back = back.reshape(STREAMS, FRAMES, TOP, D).astype(jnp.float32)
    result = mixed.astype(jnp.float32) + gate0[:, :, None] * back[:, :, 0] + gate1[:, :, None] * back[:, :, 1]
    return result.astype(jnp.bfloat16)
```

```python
import jax
import jax.numpy as jnp
from jax import lax
from jax.experimental import pallas as pl
from jax.experimental.pallas import tpu as pltpu
from jax.sharding import PartitionSpec as P

HEAD_DIM = 64
MESH = pl.DeviceIdType.MESH
BF = jnp.bfloat16
F32 = jnp.float32

NX, NZ, NY = 4, 8, 4
NE = NX * NZ
F = 256
D = 1024
H = 512
R = 16
CAP = 20
X = 256
epsilon = 1e-05


def layer_norm(values, gain):
    mean = jnp.mean(values, axis=-1, keepdims=True)
    centred = values - mean
    spread = jnp.mean(centred * centred, axis=-1, keepdims=True)
    return centred * lax.rsqrt(spread + epsilon) * gain


def dot(a, b):
    return jnp.dot(a, b, preferred_element_type=F32)


def iota(shape, dim):
    return lax.broadcasted_iota(jnp.int32, shape, dim)


def onehot(mask):
    return jnp.where(mask, 1.0, 0.0).astype(BF)


def kernel(
    keep,
    ids,
    ids_t,
    gains,
    router,
    frames,
    qkv,
    wo,
    win,
    wout,
    out,
    pbuf,
    strm,
    normed,
    wall,
    wo_sib,
    proj,
    ctxh,
    ctxs,
    mixed,
    tx,
    rx,
    ry,
    fx,
    xr,
    acc,
    win_all,
    wout_all,
    pick,
    pick_x,
    ring_s,
    ring_r,
    w_s,
    w_r,
    m_s,
    m_r,
    t_s,
    t_r,
    f_s,
    f_r,
    loc,
):
    dp = lax.axis_index("dp")
    ex = lax.axis_index("expert")
    y, c = lax.div(dp, 2), lax.rem(dp, 2)
    z, x = lax.div(ex, NX), lax.rem(ex, NX)
    sib = y * 2 + (1 - c)

    def at_y(step):
        return lax.rem(y + (step + NY), NY) * 2 + c

    def at_z(step):
        return lax.rem(z + (step + NZ), NZ)

    def at_x(step):
        return lax.rem(x + (step + NX), NX)

    def remote(src, dst, send, recv, to):
        return pltpu.make_async_remote_copy(
            src_ref=src,
            dst_ref=dst,
            send_sem=send,
            recv_sem=recv,
            device_id=to,
            device_id_type=MESH,
        )

    half = pl.ds(pl.multiple_of(c * H, 128), H)
    mine = [
        pltpu.make_async_copy(qkv.at[:, :, half], wall.at[pl.ds(0, 3), z, x], loc.at[0]),
        pltpu.make_async_copy(wo.at[:, half], wall.at[3, z, x], loc.at[1]),
        pltpu.make_async_copy(win, win_all.at[dp], loc.at[2]),
        pltpu.make_async_copy(wout, wout_all.at[dp], loc.at[3]),
    ]
    for copy in mine:
        copy.start()

    swap = remote(frames, pbuf, m_s.at[0], m_r.at[0], (at_y(2), ex))
    swap.start()

    def ring(count, base, view, step_at, device):
        last = count // 2

        def pair(step):
            r, l = step_at(-(step - 1)), step_at(step - 1)
            if step == last:
                right, left = view(r, 0, 2), view(l, 2, 2)
            else:
                right, left = view(r, 0, 4), view(l, 0, 4)
            i = base + 2 * (step - 1)
            return (
                remote(right, right, ring_s.at[i], ring_r.at[i], device(1)),
                remote(left, left, ring_s.at[i + 1], ring_r.at[i + 1], device(-1)),
            )

        def arrived(step):
            r, l = step_at(-step), step_at(step)
            if step == last:
                right, left = view(r, 0, 2), view(l, 2, 2)
            else:
                right, left = view(r, 0, 4), view(l, 0, 4)
            i = base + 2 * (step - 1)
            return (
                remote(right, right, ring_s.at[i], ring_r.at[i], device(1)),
                remote(left, left, ring_s.at[i + 1], ring_r.at[i + 1], device(-1)),
            )

        def begin(step):
            for copy in pair(step):
                copy.start()

        def wait(step):
            for copy in arrived(step):
                copy.wait_recv()

        def finish():
            for step in range(1, last + 1):
                for copy in pair(step):
                    copy.wait_send()

        return begin, wait, finish, last

    def to_x(step):
        return (dp, z * NX + at_x(step))

    def to_z(step):
        return (dp, at_z(step) * NX + x)

    x_small = ring(NX, 0, lambda k, a, n: wall.at[pl.ds(a, n), z, k], at_x, to_x)
    z_large = ring(NZ, 4, lambda k, a, n: wall.at[pl.ds(a, n), k], at_z, to_z)
    z_small = ring(NZ, 4, lambda k, a, n: wall.at[pl.ds(a, n), k, x], at_z, to_z)
    x_large = ring(NX, 0, lambda k, a, n: wall.at[pl.ds(a, n), :, k], at_x, to_x)

    mine[0].wait()
    mine[1].wait()

    @pl.when(c == 0)
    def _():
        x_small[0](1)

    @pl.when(c == 1)
    def _():
        z_small[0](1)

    def w_in(kind, block, to):
        return remote(win_all.at[block], win_all.at[block], w_s.at[kind], w_r.at[kind], (to, ex))

    def w_out(kind, block, to):
        return remote(wout_all.at[block], wout_all.at[block], w_s.at[kind], w_r.at[kind], (to, ex))

    right, left = at_y(1), at_y(-1)
    mine[2].wait()
    mine[3].wait()
    weights = [
        w_in(0, dp, right),
        w_out(3, dp, left),
        w_out(1, dp, right),
        w_in(2, dp, left),
        w_in(4, dp, sib),
        w_out(5, dp, sib),
    ]
    for copy in weights:
        copy.start()

    @pl.when(c == 0)
    def _():
        for step in range(1, x_small[3]):
            x_small[1](step)
            x_small[0](step + 1)
        x_small[1](x_small[3])
        z_large[0](1)

    @pl.when(c == 1)
    def _():
        for step in range(1, z_small[3]):
            z_small[1](step)
            z_small[0](step + 1)
        z_small[1](z_small[3])
        x_large[0](1)

    named = (ids_t[0:1, :] == iota((NE, F), 0)) | (ids_t[1:2, :] == iota((NE, F), 0))
    before = onehot(iota((F, F), 0) < iota((F, F), 1))
    rank = jnp.where(named, dot(onehot(named), before), -1.0).astype(BF)
    rows = NE * R
    spread = onehot(lax.div(iota((rows, NE), 0), R) == iota((rows, NE), 1))
    rank = dot(spread, rank)
    slot = iota((rows, F), 0)
    pick[...] = onehot(rank == lax.rem(slot, R).astype(F32))
    pick_x[...] = onehot(rank == (lax.rem(slot, 4) + R).astype(F32))

    swap.wait_recv()
    stay = keep[0:1, 0:1] > 0.5
    stream = jnp.where(stay, frames[...].astype(F32), pbuf[...].astype(F32))
    strm[...] = stream.astype(BF)
    normed[c] = layer_norm(stream, gains[0:1, :]).astype(BF)
    share = remote(normed.at[c], normed.at[c], m_s.at[1], m_r.at[1], (sib, ex))
    share.start()

    @pl.when(c == 0)
    def _():
        for step in range(1, z_large[3]):
            z_large[1](step)
            z_large[0](step + 1)
        z_large[1](z_large[3])
        x_small[2]()
        z_large[2]()

    @pl.when(c == 1)
    def _():
        for step in range(1, x_large[3]):
            x_large[1](step)
            x_large[0](step + 1)
        x_large[1](x_large[3])
        z_small[2]()
        x_large[2]()

    give_wo = remote(wall.at[3], wo_sib, m_s.at[2], m_r.at[2], (sib, ex))
    give_wo.start()
    remote(
        normed.at[1 - c], normed.at[1 - c], m_s.at[1], m_r.at[1], (sib, ex)
    ).wait_recv()

    @pl.loop(0, 3)
    def _(m):
        w = wall[m].reshape(D, H)
        for s in range(2):
            proj[m, s] = dot(normed[s], w).astype(BF)

    lane = iota((F, 128), 1)

    def attend(s, store):
        @pl.loop(0, H // 128)
        def _(h):
            cols = pl.ds(pl.multiple_of(h * 128, 128), 128)
            q = proj[0, s, :, cols] * jnp.asarray(HEAD_DIM**-0.5, BF)
            k = proj[1, s, :, cols]
            v = proj[2, s, :, cols]
            zero = jnp.zeros_like(q)
            for_both = jnp.concatenate(
                [jnp.where(lane < HEAD_DIM, q, zero), jnp.where(lane < HEAD_DIM, zero, q)], axis=0
            )
            scores = lax.dot_general(
                for_both, k, (((1,), (1,)), ((), ())), preferred_element_type=F32
            )
            scores = jnp.exp(scores - jnp.max(scores, axis=-1, keepdims=True))
            probs = (scores / jnp.sum(scores, axis=-1, keepdims=True)).astype(BF)
            both = dot(probs, v)
            store(cols, jnp.where(lane < HEAD_DIM, both[:F], both[F:]).astype(BF))

    def store_other(cols, value):
        ctxs[:, cols] = value

    def store_own(cols, value):
        ctxh[c, :, cols] = value

    attend(1 - c, store_other)
    give_ctx = remote(ctxs, ctxh.at[c], m_s.at[3], m_r.at[3], (sib, ex))
    give_ctx.start()
    attend(c, store_own)
    remote(wo_sib, wo_sib, m_s.at[2], m_r.at[2], (sib, ex)).wait_recv()
    remote(
        ctxh.at[1 - c], ctxh.at[1 - c], m_s.at[3], m_r.at[3], (sib, ex)
    ).wait_recv()

    def project(w):
        return dot(ctxh[0], w[:H]) + dot(ctxh[1], w[H:])

    other = pl.ds(pl.multiple_of((1 - c) * H, 128), H)
    mixed[:, half] = (strm[:, half].astype(F32) + project(wall[3].reshape(D, H))).astype(BF)
    mixed[:, other] = (strm[:, other].astype(F32) + project(wo_sib[...].reshape(D, H))).astype(BF)
    normed2 = layer_norm(mixed[...].astype(F32), gains[1:2, :]).astype(BF)

    tx[:, :, 0:D] = dot(pick[...], normed2).astype(BF).reshape(NE, R, D)
    tail = dot(pick_x[...], normed2)
    part = lax.div(lax.rem(iota((rows, X), 0), R), 4)
    packed = tail[:, 0:X]
    for p in range(1, 4):
        packed = jnp.where(part == p, tail[:, p * X : (p + 1) * X], packed)
    tx[:, :, D : D + X] = packed.astype(BF).reshape(NE, R, X)

    def away(k):
        return lax.rem(z + lax.div(k, NX), NZ) * NX + lax.rem(x + lax.rem(k, NX), NX)

    def back(k):
        return lax.rem(z + NZ - lax.div(k, NX), NZ) * NX + lax.rem(x + NX - lax.rem(k, NX), NX)

    def send_out(k):
        to = away(k)
        return remote(tx.at[to], rx.at[ex], t_s.at[k], t_r.at[k], (dp, to))

    def came_in(k):
        src = back(k)
        return remote(rx.at[src], rx.at[src], t_s.at[k], t_r.at[k], (dp, src))

    def give_back(k):
        to = back(k)
        return remote(ry.at[to], fx.at[ex], f_s.at[k], f_r.at[k], (dp, to))

    def got_back(k):
        src = away(k)
        return remote(fx.at[src], fx.at[src], f_s.at[k], f_r.at[k], (dp, src))

    @pl.loop(1, NE)
    def _(k):
        send_out(k).start()

    rx[ex] = tx[ex]

    r0 = router[...].astype(BF)
    r1 = (router[...] - r0.astype(F32)).astype(BF)
    r2 = (router[...] - r0.astype(F32) - r1.astype(F32)).astype(BF)
    logits = dot(normed2, r0) + (dot(normed2, r1) + dot(normed2, r2))
    expert = iota((F, NE), 1)
    first, second = ids[:, 0:1] == expert, ids[:, 1:2] == expert
    zero = jnp.zeros_like(logits)
    ahead = jnp.sum(jnp.where(first, logits, zero), axis=1, keepdims=True) - jnp.sum(
        jnp.where(second, logits, zero), axis=1, keepdims=True
    )
    gate = 1.0 / (1.0 + jnp.exp(-ahead))
    gates = jnp.where(first, gate, jnp.where(second, 1.0 - gate, zero))
    either = onehot(first | second)
    earlier = onehot(iota((F, F), 1) < iota((F, F), 0))
    rank_f = jnp.where(first | second, dot(earlier, either), -1.0).astype(BF)
    spread_f = onehot(lax.div(iota((NE, rows), 1), R) == iota((NE, rows), 0))
    rank_f = dot(rank_f, spread_f)
    gates_hi = gates.astype(BF)
    gates_lo = (gates - gates_hi.astype(F32)).astype(BF)
    gates_hi, gates_lo = dot(gates_hi, spread_f), dot(gates_lo, spread_f)
    slot_f = iota((F, rows), 1)

    def go_on(kind, make, block, to):
        copy = make(kind, block, to)
        copy.start()
        weights.append(copy)

    w_in(0, left, right).wait_recv()
    go_on(6, w_in, left, right)
    go_on(8, w_in, left, sib)
    w_out(3, right, left).wait_recv()
    go_on(7, w_out, right, left)
    go_on(9, w_out, right, sib)
    w_out(1, left, right).wait_recv()
    go_on(10, w_out, left, sib)
    w_in(2, right, left).wait_recv()
    go_on(11, w_in, right, sib)

    @pl.loop(1, NE)
    def _(k):
        came_in(k).wait_recv()

    xr[0:rows] = rx[:, :, 0:D].reshape(rows, D)
    extra = rx[:, :, D : D + X].reshape(rows, X)
    more = NE * 4

    def unpack(p):
        i, j = iota((more, rows), 1), iota((more, rows), 0)
        return onehot(
            (lax.div(i, R) == lax.div(j, 4)) & (lax.rem(i, R) == 4 * p + lax.rem(j, 4))
        )

    for p in range(4):
        xr[rows : rows + more, p * X : (p + 1) * X] = dot(unpack(p), extra).astype(BF)

    total = rows + more
    tile = total // 2

    def expert_slice(d, begin):
        @pl.loop(0, total // tile)
        def _(t):
            at = pl.ds(pl.multiple_of(t * tile, 16), tile)
            v = dot(xr[at], win_all[d])
            hidden = (0.5 * v * (1.0 + jnp.tanh(0.5 * v))).astype(BF)
            partial = dot(hidden, wout_all[d])
            if begin:
                acc[at] = partial
            else:
                acc[at] = acc[at] + partial

    far = at_y(2)

    def of_sib(d):
        return d + (1 - 2 * c)

    expert_slice(dp, True)
    w_in(4, sib, sib).wait_recv()
    w_out(5, sib, sib).wait_recv()
    expert_slice(sib, False)
    expert_slice(left, False)
    expert_slice(right, False)
    w_in(8, of_sib(left), sib).wait_recv()
    w_out(10, of_sib(left), sib).wait_recv()
    expert_slice(of_sib(left), False)
    w_in(11, of_sib(right), sib).wait_recv()
    w_out(9, of_sib(right), sib).wait_recv()
    expert_slice(of_sib(right), False)
    w_in(6, far, right).wait_recv()
    go_on(12, w_in, far, sib)
    w_out(7, far, left).wait_recv()
    go_on(13, w_out, far, sib)
    expert_slice(far, False)
    w_in(12, of_sib(far), sib).wait_recv()
    w_out(13, of_sib(far), sib).wait_recv()
    expert_slice(of_sib(far), False)

    ry[:, :, 0:D] = acc[0:rows].astype(BF).reshape(NE, R, D)
    packed = None
    for p in range(4):
        piece = lax.dot_general(
            unpack(p),
            acc[rows : rows + more, p * X : (p + 1) * X].astype(BF),
            (((0,), (0,)), ((), ())),
            preferred_element_type=F32,
        )
        packed = piece if packed is None else packed + piece
    ry[:, :, D : D + X] = packed.astype(BF).reshape(NE, R, X)

    @pl.loop(1, NE)
    def _(k):
        give_back(k).start()

    fx[ex] = ry[ex]
    in_place = rank_f == lax.rem(slot_f, R).astype(F32)
    in_tail = rank_f == (lax.rem(slot_f, 4) + R).astype(F32)
    quarter = lax.div(lax.rem(slot_f, R), 4)

    def on(mask, values):
        return jnp.where(mask, values, 0.0).astype(BF)

    main_hi, main_lo = on(in_place, gates_hi), on(in_place, gates_lo)

    @pl.loop(1, NE)
    def _(k):
        got_back(k).wait_recv()

    last = fx[:, :, D : D + X].reshape(rows, X)
    for p in range(4):
        cols = slice(p * X, (p + 1) * X)
        body = fx[:, :, cols].reshape(rows, X)
        here = in_tail & (quarter == p)
        out[:, cols] = (
            mixed[:, cols].astype(F32)
            + (dot(main_hi, body) + dot(on(here, gates_hi), last))
            + (dot(main_lo, body) + dot(on(here, gates_lo), last))
        ).astype(BF)

    @pl.loop(1, NE)
    def _(k):
        send_out(k).wait_send()
        give_back(k).wait_send()

    for copy in weights + [swap, share, give_wo, give_ctx]:
        copy.wait_send()


def body(
    frames_in, pit_order, expert_ids, norm_gains, attn_qkv, attn_out, router, expert_in, expert_out
):
    dp_index = lax.axis_index("dp")
    exp_index = lax.axis_index("expert")
    speaker = dp_index // (NY * 2 // 2)
    meeting = dp_index % NY * NE + exp_index
    keep = (pit_order[meeting, speaker] == speaker).astype(F32)
    keep = jnp.broadcast_to(keep, (8, 128))
    ids = expert_ids[0]
    vmem = pl.BlockSpec(memory_space=pltpu.VMEM)
    hbm = pl.BlockSpec(memory_space=pl.ANY)
    dma = pltpu.SemaphoreType.DMA
    rows = NE * R
    out = pl.pallas_call(
        kernel,
        out_shape=jax.ShapeDtypeStruct((F, D), BF),
        in_specs=[vmem] * 6 + [hbm] * 4,
        out_specs=vmem,
        scratch_shapes=[
            pltpu.VMEM((F, D), BF),
            pltpu.VMEM((F, D), BF),
            pltpu.VMEM((2, F, D), BF),
            pltpu.VMEM((4, NZ, NX, D // NE, H), BF),
            pltpu.VMEM((NZ, NX, D // NE, H), BF),
            pltpu.VMEM((3, 2, F, H), BF),
            pltpu.VMEM((2, F, H), BF),
            pltpu.VMEM((F, H), BF),
            pltpu.VMEM((F, D), BF),
            pltpu.VMEM((NE, R, D + X), BF),
            pltpu.VMEM((NE, R, D + X), BF),
            pltpu.VMEM((NE, R, D + X), BF),
            pltpu.VMEM((NE, R, D + X), BF),
            pltpu.VMEM((NE * CAP, D), BF),
            pltpu.VMEM((NE * CAP, D), F32),
            pltpu.VMEM((2 * NY, D, H), BF),
            pltpu.VMEM((2 * NY, H, D), BF),
            pltpu.VMEM((rows, F), BF),
            pltpu.VMEM((rows, F), BF),
            dma((12,)),
            dma((12,)),
            dma((14,)),
            dma((14,)),
            dma((4,)),
            dma((4,)),
            dma((NE,)),
            dma((NE,)),
            dma((NE,)),
            dma((NE,)),
            dma((4,)),
        ],
        compiler_params=pltpu.CompilerParams(
            has_side_effects=True, vmem_limit_bytes=60 * 2**20
        ),
        cost_estimate=pl.CostEstimate(
            flops=14 * 10**9, bytes_accessed=8 * 2**20, transcendentals=4 * 10**6
        ),
    )(
        keep,
        ids,
        ids.T,
        norm_gains,
        router,
        frames_in[0],
        attn_qkv,
        attn_out,
        expert_in[0],
        expert_out[0],
    )
    return out[None]


def solution(mesh):
    return jax.shard_map(
        body,
        mesh=mesh,
        in_specs=(
            P(("dp", "expert"), None, None),
            P(),
            P(("dp", "expert"), None, None),
            P(),
            P(None, "expert", None),
            P("expert", None),
            P(),
            P("expert", None, "dp"),
            P("expert", "dp", None),
        ),
        out_specs=P(("dp", "expert"), None, None),
        check_vma=False,
    )
```

```python
import functools

import jax
import jax.numpy as jnp
from jax import lax
from jax.experimental import pallas as pl
from jax.experimental.pallas import tpu as pltpu
from jax.sharding import PartitionSpec as P

HEAD_DIM = 64
MESH = pl.DeviceIdType.MESH
BF = jnp.bfloat16
F32 = jnp.float32

NX, NZ, NY = 4, 8, 4
NE = NX * NZ
F = 256
D = 1024
H = 512
R = 16
CAP = 20
X = 256
MEETINGS = 128
epsilon = 1e-05


def layer_norm(values, gain):
    mean = jnp.mean(values, axis=-1, keepdims=True)
    centred = values - mean
    spread = jnp.mean(centred * centred, axis=-1, keepdims=True)
    return centred * lax.rsqrt(spread + epsilon) * gain


def dot(a, b):
    return jnp.dot(a, b, preferred_element_type=F32)


def iota(shape, dim):
    return lax.broadcasted_iota(jnp.int32, shape, dim)


def onehot(mask):
    return jnp.where(mask, 1.0, 0.0).astype(BF)


def kernel(
    order,
    ids_t,
    gains,
    router,
    frames,
    qkv,
    wo,
    win,
    wout,
    out,
    pbuf,
    strm,
    normed,
    wall,
    wo_sib,
    proj,
    ctxh,
    ctxs,
    mixed,
    tx,
    rx,
    ry,
    fx,
    xr,
    acc,
    win_all,
    wout_all,
    pick,
    pick_x,
    ring_s,
    ring_r,
    w_s,
    w_r,
    m_s,
    m_r,
    t_s,
    t_r,
    f_s,
    f_r,
    loc,
):
    dp = lax.axis_index("dp")
    ex = lax.axis_index("expert")
    y, c = lax.div(dp, 2), lax.rem(dp, 2)
    z, x = lax.div(ex, NX), lax.rem(ex, NX)
    sib = y * 2 + (1 - c)

    def at_y(step):
        return lax.rem(y + (step + NY), NY) * 2 + c

    def at_z(step):
        return lax.rem(z + (step + NZ), NZ)

    def at_x(step):
        return lax.rem(x + (step + NX), NX)

    def remote(src, dst, send, recv, to):
        return pltpu.make_async_remote_copy(
            src_ref=src,
            dst_ref=dst,
            send_sem=send,
            recv_sem=recv,
            device_id=to,
            device_id_type=MESH,
        )

    barrier = pltpu.get_barrier_semaphore()

    def greet(to):
        pl.semaphore_signal(barrier, inc=1, device_id=to, device_id_type=MESH)

    for to in (at_y(1), at_y(-1), at_y(2), sib):
        greet((to, ex))

    @pl.loop(1, NE)
    def _(k):
        greet((dp, lax.rem(ex + k, NE)))

    half = pl.ds(pl.multiple_of(c * H, 128), H)
    mine = [
        pltpu.make_async_copy(qkv.at[:, :, half], wall.at[pl.ds(0, 3), z, x], loc.at[0]),
        pltpu.make_async_copy(wo.at[:, half], wall.at[3, z, x], loc.at[1]),
        pltpu.make_async_copy(win, win_all.at[dp], loc.at[2]),
        pltpu.make_async_copy(wout, wout_all.at[dp], loc.at[3]),
    ]
    for copy in mine:
        copy.start()
    pl.semaphore_wait(barrier, NE - 1 + 4)

    swap = remote(frames, pbuf, m_s.at[0], m_r.at[0], (at_y(2), ex))
    swap.start()

    class Ring:
        def __init__(self, count, base, view, step_at, device):
            self.last = count // 2
            self.base, self.view, self.step_at, self.device = base, view, step_at, device

        def pair(self, step, hop):
            last = step == self.last
            right = self.view(self.step_at(hop - step), pl.ds(0, H // 2 if last else H))
            left = self.view(self.step_at(step - hop), pl.ds(H // 2 if last else 0, H // 2 if last else H))
            i = self.base + 2 * (step - 1)
            return (
                remote(right, right, ring_s.at[i], ring_r.at[i], self.device(1)),
                remote(left, left, ring_s.at[i + 1], ring_r.at[i + 1], self.device(-1)),
            )

        def begin(self, step):
            for copy in self.pair(step, 1):
                copy.start()

        def wait(self, step):
            for copy in self.pair(step, 0):
                copy.wait_recv()

        def relay(self, step):
            self.wait(step)
            if step < self.last:
                self.begin(step + 1)

        def finish(self):
            for step in range(1, self.last + 1):
                for copy in self.pair(step, 1):
                    copy.wait_send()

    def to_x(step):
        return (dp, z * NX + at_x(step))

    def to_z(step):
        return (dp, at_z(step) * NX + x)

    chunks = ((0, 2), (2, 1), (3, 1))
    small, large = {0: [], 1: []}, {0: [], 1: []}
    for i, (m, n) in enumerate(chunks):
        mats = pl.ds(m, n)
        bx, bz = 12 * i, 12 * i + 4
        small[0].append(Ring(NX, bx, lambda k, w, mats=mats: wall.at[mats, z, k, :, w], at_x, to_x))
        large[0].append(Ring(NZ, bz, lambda k, w, mats=mats: wall.at[mats, k, :, :, w], at_z, to_z))
        small[1].append(Ring(NZ, bz, lambda k, w, mats=mats: wall.at[mats, k, x, :, w], at_z, to_z))
        large[1].append(Ring(NX, bx, lambda k, w, mats=mats: wall.at[mats, :, k, :, w], at_x, to_x))

    mine[0].wait()
    mine[1].wait()

    def on_core(core, work):
        pl.when(c == core)(functools.partial(work, small[core], large[core]))

    def start_small(small, large):
        for ring in small:
            ring.begin(1)

    on_core(0, start_small)
    on_core(1, start_small)

    def small_to_large(small, large):
        for step in range(1, small[0].last):
            for ring in small:
                ring.relay(step)
        for near, wide in zip(small, large):
            near.wait(near.last)
            if wide is not large[-1]:
                wide.begin(1)

    on_core(0, small_to_large)
    on_core(1, small_to_large)

    def w_in(kind, block, to):
        return remote(win_all.at[block], win_all.at[block], w_s.at[kind], w_r.at[kind], (to, ex))

    def w_out(kind, block, to):
        return remote(wout_all.at[block], wout_all.at[block], w_s.at[kind], w_r.at[kind], (to, ex))

    right, left = at_y(1), at_y(-1)
    mine[2].wait()
    mine[3].wait()
    weights = [
        w_in(0, dp, right),
        w_out(3, dp, left),
        w_out(1, dp, right),
        w_in(2, dp, left),
        w_in(4, dp, sib),
        w_out(5, dp, sib),
    ]
    for copy in weights:
        copy.start()

    named = (ids_t[0:1, :] == iota((NE, F), 0)) | (ids_t[1:2, :] == iota((NE, F), 0))
    before = onehot(iota((F, F), 0) < iota((F, F), 1))
    rank = jnp.where(named, dot(onehot(named), before), -1.0).astype(BF)
    rows = NE * R
    spread = onehot(lax.div(iota((rows, NE), 0), R) == iota((rows, NE), 1))
    rank = dot(spread, rank)
    slot = iota((rows, F), 0)
    pick[...] = onehot(rank == lax.rem(slot, R).astype(F32))
    pick_x[...] = onehot(rank == (lax.rem(slot, 4) + R).astype(F32))

    swap.wait_recv()
    speaker = lax.div(y, NY // 2)
    meeting = lax.rem(dp, NY) * NE + ex
    here = (iota((2, MEETINGS), 0) == speaker) & (iota((2, MEETINGS), 1) == meeting)
    source = jnp.sum(jnp.where(here, order[...], 0).astype(F32), axis=(0, 1), keepdims=True)
    stay = source == speaker.astype(F32)
    stream = jnp.where(stay, frames[...].astype(F32), pbuf[...].astype(F32))
    strm[...] = stream.astype(BF)
    normed[c] = layer_norm(stream, gains[0:1, :]).astype(BF)
    share = remote(normed.at[c], normed.at[c], m_s.at[1], m_r.at[1], (sib, ex))
    share.start()

    def most(small, large):
        for step in range(1, large[0].last):
            for ring in large[:2]:
                ring.relay(step)
        large[0].wait(large[0].last)
        large[2].begin(1)

    def values(small, large):
        large[1].wait(large[1].last)

    def output(step, small, large):
        if step <= large[2].last:
            large[2].relay(step)

    def go_round(step):
        on_core(0, functools.partial(output, step))
        on_core(1, functools.partial(output, step))

    on_core(0, most)
    on_core(1, most)
    remote(
        normed.at[1 - c], normed.at[1 - c], m_s.at[1], m_r.at[1], (sib, ex)
    ).wait_recv()

    for m in range(3):
        if m == 2:
            on_core(0, values)
            on_core(1, values)
        w = wall[m].reshape(D, H)
        for s in range(2):
            proj[m, s] = dot(normed[s], w).astype(BF)
        go_round(m + 1)

    lane = iota((F, 128), 1)

    def attend(s, store):
        @pl.loop(0, H // 128)
        def _(h):
            cols = pl.ds(pl.multiple_of(h * 128, 128), 128)
            q = proj[0, s, :, cols] * jnp.asarray(HEAD_DIM**-0.5, BF)
            k = proj[1, s, :, cols]
            v = proj[2, s, :, cols]
            zero = jnp.zeros_like(q)
            for_both = jnp.concatenate(
                [jnp.where(lane < HEAD_DIM, q, zero), jnp.where(lane < HEAD_DIM, zero, q)], axis=0
            )
            scores = lax.dot_general(
                for_both, k, (((1,), (1,)), ((), ())), preferred_element_type=F32
            )
            scores = jnp.exp(scores - jnp.max(scores, axis=-1, keepdims=True))
            probs = (scores / jnp.sum(scores, axis=-1, keepdims=True)).astype(BF)
            both = dot(probs, v)
            store(cols, jnp.where(lane < HEAD_DIM, both[:F], both[F:]).astype(BF))

    def store_other(cols, value):
        ctxs[:, cols] = value

    def store_own(cols, value):
        ctxh[c, :, cols] = value

    attend(1 - c, store_other)
    go_round(4)
    give_wo = remote(wall.at[3], wo_sib, m_s.at[2], m_r.at[2], (sib, ex))
    give_wo.start()
    give_ctx = remote(ctxs, ctxh.at[c], m_s.at[3], m_r.at[3], (sib, ex))
    give_ctx.start()
    attend(c, store_own)
    remote(wo_sib, wo_sib, m_s.at[2], m_r.at[2], (sib, ex)).wait_recv()
    remote(
        ctxh.at[1 - c], ctxh.at[1 - c], m_s.at[3], m_r.at[3], (sib, ex)
    ).wait_recv()

    def project(w):
        return dot(ctxh[0], w[:H]) + dot(ctxh[1], w[H:])

    other = pl.ds(pl.multiple_of((1 - c) * H, 128), H)
    mixed[:, half] = (strm[:, half].astype(F32) + project(wall[3].reshape(D, H))).astype(BF)
    mixed[:, other] = (strm[:, other].astype(F32) + project(wo_sib[...].reshape(D, H))).astype(BF)
    normed2 = layer_norm(mixed[...].astype(F32), gains[1:2, :]).astype(BF)

    tx[:, :, 0:D] = dot(pick[...], normed2).astype(BF).reshape(NE, R, D)
    tail = dot(pick_x[...], normed2)
    part = lax.div(lax.rem(iota((rows, X), 0), R), 4)
    packed = tail[:, 0:X]
    for p in range(1, 4):
        packed = jnp.where(part == p, tail[:, p * X : (p + 1) * X], packed)
    tx[:, :, D : D + X] = packed.astype(BF).reshape(NE, R, X)

    def away(k):
        return lax.rem(z + lax.div(k, NX), NZ) * NX + lax.rem(x + lax.rem(k, NX), NX)

    def back(k):
        return lax.rem(z + NZ - lax.div(k, NX), NZ) * NX + lax.rem(x + NX - lax.rem(k, NX), NX)

    def send_out(k):
        to = away(k)
        return remote(tx.at[to], rx.at[ex], t_s.at[k], t_r.at[k], (dp, to))

    def came_in(k):
        src = back(k)
        return remote(rx.at[src], rx.at[src], t_s.at[k], t_r.at[k], (dp, src))

    def give_back(k):
        to = back(k)
        return remote(ry.at[to], fx.at[ex], f_s.at[k], f_r.at[k], (dp, to))

    def got_back(k):
        src = away(k)
        return remote(fx.at[src], fx.at[src], f_s.at[k], f_r.at[k], (dp, src))

    @pl.loop(1, NE)
    def _(k):
        send_out(k).start()

    rx[ex] = tx[ex]

    r0 = router[...].astype(BF)
    r1 = (router[...] - r0.astype(F32)).astype(BF)
    r2 = (router[...] - r0.astype(F32) - r1.astype(F32)).astype(BF)

    def along(b):
        return lax.dot_general(normed2, b, (((1,), (1,)), ((), ())), preferred_element_type=F32)

    logits = along(r0) + (along(r1) + along(r2))
    expert = iota((F, NE), 1)
    chosen = jnp.concatenate([ids_t[...], jnp.zeros((6, F), jnp.int32)], axis=0).astype(F32).T
    chosen = chosen.astype(jnp.int32)
    first, second = chosen[:, 0:1] == expert, chosen[:, 1:2] == expert
    zero = jnp.zeros_like(logits)
    ahead = jnp.sum(jnp.where(first, logits, zero), axis=1, keepdims=True) - jnp.sum(
        jnp.where(second, logits, zero), axis=1, keepdims=True
    )
    gate = 1.0 / (1.0 + jnp.exp(-ahead))
    gates = jnp.where(first, gate, jnp.where(second, 1.0 - gate, zero))
    either = onehot(first | second)
    earlier = onehot(iota((F, F), 1) < iota((F, F), 0))
    rank_f = jnp.where(first | second, dot(earlier, either), -1.0).astype(BF)
    spread_f = onehot(lax.div(iota((NE, rows), 1), R) == iota((NE, rows), 0))
    rank_f = dot(rank_f, spread_f)
    gates_hi = gates.astype(BF)
    gates_lo = (gates - gates_hi.astype(F32)).astype(BF)
    gates_hi, gates_lo = dot(gates_hi, spread_f), dot(gates_lo, spread_f)
    slot_f = iota((F, rows), 1)

    def go_on(kind, make, block, to):
        copy = make(kind, block, to)
        copy.start()
        weights.append(copy)

    w_in(0, left, right).wait_recv()
    go_on(6, w_in, left, right)
    go_on(8, w_in, left, sib)
    w_out(3, right, left).wait_recv()
    go_on(7, w_out, right, left)
    go_on(9, w_out, right, sib)
    w_out(1, left, right).wait_recv()
    go_on(10, w_out, left, sib)
    w_in(2, right, left).wait_recv()
    go_on(11, w_in, right, sib)

    @pl.loop(1, NE)
    def _(k):
        came_in(k).wait_recv()

    xr[0:rows] = rx[:, :, 0:D].reshape(rows, D)
    extra = rx[:, :, D : D + X].reshape(rows, X)
    more = NE * 4

    def unpack(p):
        i, j = iota((more, rows), 1), iota((more, rows), 0)
        return onehot(
            (lax.div(i, R) == lax.div(j, 4)) & (lax.rem(i, R) == 4 * p + lax.rem(j, 4))
        )

    for p in range(4):
        xr[rows : rows + more, p * X : (p + 1) * X] = dot(unpack(p), extra).astype(BF)

    total = rows + more
    tile = total // 2

    def expert_slice(d, begin):
        @pl.loop(0, total // tile)
        def _(t):
            at = pl.ds(pl.multiple_of(t * tile, 16), tile)
            v = dot(xr[at], win_all[d])
            hidden = (0.5 * v * (1.0 + jnp.tanh(0.5 * v))).astype(BF)
            partial = dot(hidden, wout_all[d])
            if begin:
                acc[at] = partial
            else:
                acc[at] = acc[at] + partial

    far = at_y(2)

    def of_sib(d):
        return d + (1 - 2 * c)

    expert_slice(dp, True)
    w_in(4, sib, sib).wait_recv()
    w_out(5, sib, sib).wait_recv()
    expert_slice(sib, False)
    expert_slice(left, False)
    expert_slice(right, False)
    w_in(8, of_sib(left), sib).wait_recv()
    w_out(10, of_sib(left), sib).wait_recv()
    expert_slice(of_sib(left), False)
    w_in(11, of_sib(right), sib).wait_recv()
    w_out(9, of_sib(right), sib).wait_recv()
    expert_slice(of_sib(right), False)
    w_in(6, far, right).wait_recv()
    go_on(12, w_in, far, sib)
    w_out(7, far, left).wait_recv()
    go_on(13, w_out, far, sib)
    expert_slice(far, False)
    w_in(12, of_sib(far), sib).wait_recv()
    w_out(13, of_sib(far), sib).wait_recv()
    expert_slice(of_sib(far), False)

    ry[:, :, 0:D] = acc[0:rows].astype(BF).reshape(NE, R, D)
    packed = None
    for p in range(4):
        piece = lax.dot_general(
            unpack(p),
            acc[rows : rows + more, p * X : (p + 1) * X].astype(BF),
            (((0,), (0,)), ((), ())),
            preferred_element_type=F32,
        )
        packed = piece if packed is None else packed + piece
    ry[:, :, D : D + X] = packed.astype(BF).reshape(NE, R, X)

    @pl.loop(1, NE)
    def _(k):
        give_back(k).start()

    fx[ex] = ry[ex]
    in_place = rank_f == lax.rem(slot_f, R).astype(F32)
    in_tail = rank_f == (lax.rem(slot_f, 4) + R).astype(F32)
    quarter = lax.div(lax.rem(slot_f, R), 4)

    def on(mask, values):
        return jnp.where(mask, values, 0.0).astype(BF)

    main_hi, main_lo = on(in_place, gates_hi), on(in_place, gates_lo)

    @pl.loop(1, NE)
    def _(k):
        got_back(k).wait_recv()

    last = fx[:, :, D : D + X].reshape(rows, X)
    for p in range(4):
        cols = slice(p * X, (p + 1) * X)
        body = fx[:, :, cols].reshape(rows, X)
        here = in_tail & (quarter == p)
        out[:, cols] = (
            mixed[:, cols].astype(F32)
            + (dot(main_hi, body) + dot(on(here, gates_hi), last))
            + (dot(main_lo, body) + dot(on(here, gates_lo), last))
        ).astype(BF)

    @pl.loop(1, NE)
    def _(k):
        send_out(k).wait_send()
        give_back(k).wait_send()

    for copy in weights + [swap, share, give_wo, give_ctx]:
        copy.wait_send()

    def finish(small, large):
        for ring in small + large:
            ring.finish()

    on_core(0, finish)
    on_core(1, finish)


def body(
    frames_in, pit_order, expert_ids, norm_gains, attn_qkv, attn_out, router, expert_in, expert_out
):
    vmem = pl.BlockSpec(memory_space=pltpu.VMEM)
    hbm = pl.BlockSpec(memory_space=pl.ANY)
    dma = pltpu.SemaphoreType.DMA
    rows = NE * R
    out = pl.pallas_call(
        kernel,
        out_shape=jax.ShapeDtypeStruct((F, D), BF),
        in_specs=[vmem] * 5 + [hbm] * 4,
        out_specs=vmem,
        scratch_shapes=[
            pltpu.VMEM((F, D), BF),
            pltpu.VMEM((F, D), BF),
            pltpu.VMEM((2, F, D), BF),
            pltpu.VMEM((4, NZ, NX, D // NE, H), BF),
            pltpu.VMEM((NZ, NX, D // NE, H), BF),
            pltpu.VMEM((3, 2, F, H), BF),
            pltpu.VMEM((2, F, H), BF),
            pltpu.VMEM((F, H), BF),
            pltpu.VMEM((F, D), BF),
            pltpu.VMEM((NE, R, D + X), BF),
            pltpu.VMEM((NE, R, D + X), BF),
            pltpu.VMEM((NE, R, D + X), BF),
            pltpu.VMEM((NE, R, D + X), BF),
            pltpu.VMEM((NE * CAP, D), BF),
            pltpu.VMEM((NE * CAP, D), F32),
            pltpu.VMEM((2 * NY, D, H), BF),
            pltpu.VMEM((2 * NY, H, D), BF),
            pltpu.VMEM((rows, F), BF),
            pltpu.VMEM((rows, F), BF),
            dma((36,)),
            dma((36,)),
            dma((14,)),
            dma((14,)),
            dma((4,)),
            dma((4,)),
            dma((NE,)),
            dma((NE,)),
            dma((NE,)),
            dma((NE,)),
            dma((4,)),
        ],
        compiler_params=pltpu.CompilerParams(
            collective_id=0, has_side_effects=True, vmem_limit_bytes=60 * 2**20
        ),
        cost_estimate=pl.CostEstimate(
            flops=14 * 10**9, bytes_accessed=8 * 2**20, transcendentals=4 * 10**6
        ),
    )(
        pit_order.T,
        expert_ids[0].T,
        norm_gains,
        router.T,
        frames_in[0],
        attn_qkv,
        attn_out,
        expert_in[0],
        expert_out[0],
    )
    return out[None]


def solution(mesh):
    return jax.shard_map(
        body,
        mesh=mesh,
        in_specs=(
            P(("dp", "expert"), None, None),
            P(),
            P(("dp", "expert"), None, None),
            P(),
            P(None, "expert", None),
            P("expert", None),
            P(),
            P("expert", None, "dp"),
            P("expert", "dp", None),
        ),
        out_specs=P(("dp", "expert"), None, None),
        check_vma=False,
    )
```

```python
import functools

import jax
import jax.numpy as jnp
from jax import lax
from jax.experimental import pallas as pl
from jax.experimental.pallas import tpu as pltpu
from jax.sharding import PartitionSpec as P

HEAD_DIM = 64
MESH = pl.DeviceIdType.MESH
BF = jnp.bfloat16
F32 = jnp.float32

NX, NZ, NY = 4, 8, 4
NE = NX * NZ
F = 256
D = 1024
H = 512
R = 16
CAP = 20
X = 256
MEETINGS = 128
epsilon = 1e-05


def layer_norm(values, gain):
    mean = jnp.mean(values, axis=-1, keepdims=True)
    centred = values - mean
    spread = jnp.mean(centred * centred, axis=-1, keepdims=True)
    return centred * lax.rsqrt(spread + epsilon) * gain


def dot(a, b):
    return jnp.dot(a, b, preferred_element_type=F32)


def iota(shape, dim):
    return lax.broadcasted_iota(jnp.int32, shape, dim)


def onehot(mask):
    return jnp.where(mask, 1.0, 0.0).astype(BF)


def kernel(
    order,
    ids_t,
    gains,
    router,
    frames,
    qkv,
    wo,
    win,
    wout,
    out,
    pbuf,
    strm,
    normed,
    wall,
    wo_sib,
    proj,
    ctxh,
    ctxs,
    mixed,
    tx,
    rx,
    ry,
    fx,
    xr,
    hidden,
    acc,
    win_all,
    wout_all,
    weigh,
    pick,
    pick_x,
    ring_s,
    ring_r,
    w_s,
    w_r,
    m_s,
    m_r,
    t_s,
    t_r,
    f_s,
    f_r,
    loc,
):
    dp = lax.axis_index("dp")
    ex = lax.axis_index("expert")
    y, c = lax.div(dp, 2), lax.rem(dp, 2)
    z, x = lax.div(ex, NX), lax.rem(ex, NX)
    sib = y * 2 + (1 - c)

    def at_y(step):
        return lax.rem(y + (step + NY), NY) * 2 + c

    def at_z(step):
        return lax.rem(z + (step + NZ), NZ)

    def at_x(step):
        return lax.rem(x + (step + NX), NX)

    def remote(src, dst, send, recv, to):
        return pltpu.make_async_remote_copy(
            src_ref=src,
            dst_ref=dst,
            send_sem=send,
            recv_sem=recv,
            device_id=to,
            device_id_type=MESH,
        )

    barrier = pltpu.get_barrier_semaphore()

    def greet(to):
        pl.semaphore_signal(barrier, inc=1, device_id=to, device_id_type=MESH)

    for to in (at_y(1), at_y(-1), at_y(2), sib):
        greet((to, ex))

    @pl.loop(1, NE)
    def _(k):
        greet((dp, lax.rem(ex + k, NE)))

    half = pl.ds(pl.multiple_of(c * H, 128), H)
    mine = [
        pltpu.make_async_copy(qkv.at[:, :, half], wall.at[pl.ds(0, 3), z, x], loc.at[0]),
        pltpu.make_async_copy(wo.at[:, half], wall.at[3, z, x], loc.at[1]),
        pltpu.make_async_copy(win, win_all.at[dp], loc.at[2]),
        pltpu.make_async_copy(wout.at[:, pl.ds(0, H)], wout_all.at[0, dp], loc.at[3]),
        pltpu.make_async_copy(wout.at[:, pl.ds(H, H)], wout_all.at[1, dp], loc.at[4]),
    ]
    for copy in mine:
        copy.start()
    pl.semaphore_wait(barrier, NE - 1 + 4)

    swap = remote(frames, pbuf, m_s.at[0], m_r.at[0], (at_y(2), ex))
    swap.start()

    class Ring:
        def __init__(self, count, base, view, step_at, device):
            self.last = count // 2
            self.base, self.view, self.step_at, self.device = base, view, step_at, device

        def pair(self, step, hop):
            last = step == self.last
            right = self.view(self.step_at(hop - step), pl.ds(0, H // 2 if last else H))
            left = self.view(self.step_at(step - hop), pl.ds(H // 2 if last else 0, H // 2 if last else H))
            i = self.base + 2 * (step - 1)
            return (
                remote(right, right, ring_s.at[i], ring_r.at[i], self.device(1)),
                remote(left, left, ring_s.at[i + 1], ring_r.at[i + 1], self.device(-1)),
            )

        def begin(self, step):
            for copy in self.pair(step, 1):
                copy.start()

        def wait(self, step):
            for copy in self.pair(step, 0):
                copy.wait_recv()

        def relay(self, step):
            self.wait(step)
            if step < self.last:
                self.begin(step + 1)

        def finish(self):
            for step in range(1, self.last + 1):
                for copy in self.pair(step, 1):
                    copy.wait_send()

    def to_x(step):
        return (dp, z * NX + at_x(step))

    def to_z(step):
        return (dp, at_z(step) * NX + x)

    chunks = ((0, 1), (1, 1), (2, 1), (3, 1))
    small, large = {0: [], 1: []}, {0: [], 1: []}
    for i, (m, n) in enumerate(chunks):
        mats = pl.ds(m, n)
        bx, bz = 12 * i, 12 * i + 4
        small[0].append(Ring(NX, bx, lambda k, w, mats=mats: wall.at[mats, z, k, :, w], at_x, to_x))
        large[0].append(Ring(NZ, bz, lambda k, w, mats=mats: wall.at[mats, k, :, :, w], at_z, to_z))
        small[1].append(Ring(NZ, bz, lambda k, w, mats=mats: wall.at[mats, k, x, :, w], at_z, to_z))
        large[1].append(Ring(NX, bx, lambda k, w, mats=mats: wall.at[mats, :, k, :, w], at_x, to_x))

    mine[0].wait()
    mine[1].wait()

    def on_core(core, work):
        pl.when(c == core)(functools.partial(work, small[core], large[core]))

    def start_small(small, large):
        for ring in small:
            ring.begin(1)

    on_core(0, start_small)
    on_core(1, start_small)

    named = (ids_t[0:1, :] == iota((NE, F), 0)) | (ids_t[1:2, :] == iota((NE, F), 0))
    before = onehot(iota((F, F), 0) < iota((F, F), 1))
    rank = jnp.where(named, dot(onehot(named), before), -1.0).astype(BF)
    rows = NE * R
    spread = onehot(lax.div(iota((rows, NE), 0), R) == iota((rows, NE), 1))
    rank = dot(spread, rank)
    slot = iota((rows, F), 0)
    pick[...] = onehot(rank == lax.rem(slot, R).astype(F32))
    pick_x[...] = onehot(rank == (lax.rem(slot, 4) + R).astype(F32))

    def small_to_large(small, large):
        for step in range(1, small[0].last):
            for ring in small:
                ring.relay(step)
        for near, wide in zip(small, large):
            near.wait(near.last)
            if wide is not large[-1]:
                wide.begin(1)

    on_core(0, small_to_large)
    on_core(1, small_to_large)

    right, left, far = at_y(1), at_y(-1), at_y(2)

    def of_sib(d):
        return d + (1 - 2 * c)

    sent = []

    class Chunk:
        def __init__(self, base, ref, depth):
            self.base, self.ref, self.depth = base, ref, depth

        def copy(self, kind, d, to):
            first = kind in (3, 7)
            rows = pl.ds(0 if first or kind not in (4, 8) else self.depth // 2, self.depth // 2 if kind in (3, 4, 7, 8) else self.depth)
            ref = self.ref.at[d, rows]
            i = self.base + kind
            return remote(ref, ref, w_s.at[i], w_r.at[i], (to, ex))

        def send(self, kind, d, to):
            copy = self.copy(kind, d, to)
            copy.start()
            sent.append(copy)

        def wait(self, kind, d):
            self.copy(kind, d, sib).wait_recv()

        def own(self):
            self.send(0, dp, right)
            self.send(1, dp, left)
            self.send(2, dp, sib)

        def relay(self):
            self.wait(0, left)
            self.send(3, left, right)
            self.send(5, left, sib)
            self.wait(1, right)
            self.send(4, right, left)
            self.send(6, right, sib)

        def relay_far(self):
            self.wait(3, far)
            self.send(7, far, sib)
            self.wait(4, far)
            self.send(8, far, sib)

        def from_sib(self):
            self.wait(2, sib)
            self.wait(5, of_sib(left))
            self.wait(6, of_sib(right))

        def far_from_sib(self):
            self.wait(7, of_sib(far))
            self.wait(8, of_sib(far))

    chunk_in = Chunk(0, win_all, D)
    chunk_out = [Chunk(9 * (1 + h), wout_all.at[h], H) for h in range(2)]
    for copy in mine[2:]:
        copy.wait()
    chunk_in.own()

    def most(small, large):
        steps = large[0].last
        for step in range(1, min(3, steps)):
            for ring in large[:3]:
                ring.relay(step)
            if step == 1:
                large[3].begin(1)
            else:
                large[3].relay(step - 1)

    on_core(0, most)
    on_core(1, most)

    swap.wait_recv()
    speaker = lax.div(y, NY // 2)
    meeting = lax.rem(dp, NY) * NE + ex
    here = (iota((2, MEETINGS), 0) == speaker) & (iota((2, MEETINGS), 1) == meeting)
    source = jnp.sum(jnp.where(here, order[...], 0).astype(F32), axis=(0, 1), keepdims=True)
    stay = source == speaker.astype(F32)
    stream = jnp.where(stay, frames[...].astype(F32), pbuf[...].astype(F32))
    strm[...] = stream.astype(BF)
    normed[c] = layer_norm(stream, gains[0:1, :]).astype(BF)
    share = remote(normed.at[c], normed.at[c], m_s.at[1], m_r.at[1], (sib, ex))
    share.start()

    def rest(small, large):
        for step in range(3, large[0].last):
            for ring in large[:3]:
                ring.relay(step)
            large[3].relay(step - 1)

    def come(m, small, large):
        large[m].wait(large[m].last)

    def output(steps, small, large):
        step = steps[0] if large[3].last == NZ // 2 else steps[1]
        large[3].relay(step)

    def on_both(work):
        on_core(0, work)
        on_core(1, work)

    on_both(rest)
    remote(
        normed.at[1 - c], normed.at[1 - c], m_s.at[1], m_r.at[1], (sib, ex)
    ).wait_recv()
    chunk_out[0].own()

    for m in range(3):
        on_both(functools.partial(come, m))
        w = wall[m].reshape(D, H)
        for s in range(2):
            proj[m, s] = dot(normed[s], w).astype(BF)
        if m == 1:
            on_both(functools.partial(output, (3, 1)))

    lane = iota((F, 128), 1)

    def attend(s, store):
        @pl.loop(0, H // 128)
        def _(h):
            cols = pl.ds(pl.multiple_of(h * 128, 128), 128)
            q = proj[0, s, :, cols] * jnp.asarray(HEAD_DIM**-0.5, BF)
            k = proj[1, s, :, cols]
            v = proj[2, s, :, cols]
            zero = jnp.zeros_like(q)
            for_both = jnp.concatenate(
                [jnp.where(lane < HEAD_DIM, q, zero), jnp.where(lane < HEAD_DIM, zero, q)], axis=0
            )
            scores = lax.dot_general(
                for_both, k, (((1,), (1,)), ((), ())), preferred_element_type=F32
            )
            scores = jnp.exp(scores - jnp.max(scores, axis=-1, keepdims=True))
            probs = (scores / jnp.sum(scores, axis=-1, keepdims=True)).astype(BF)
            both = dot(probs, v)
            store(cols, jnp.where(lane < HEAD_DIM, both[:F], both[F:]).astype(BF))

    def store_other(cols, value):
        ctxs[:, cols] = value

    def store_own(cols, value):
        ctxh[c, :, cols] = value

    attend(1 - c, store_other)
    on_both(functools.partial(output, (4, 2)))
    give_wo = remote(wall.at[3], wo_sib, m_s.at[2], m_r.at[2], (sib, ex))
    give_wo.start()
    give_ctx = remote(ctxs, ctxh.at[c], m_s.at[3], m_r.at[3], (sib, ex))
    give_ctx.start()
    attend(c, store_own)
    remote(wo_sib, wo_sib, m_s.at[2], m_r.at[2], (sib, ex)).wait_recv()
    remote(
        ctxh.at[1 - c], ctxh.at[1 - c], m_s.at[3], m_r.at[3], (sib, ex)
    ).wait_recv()

    def project(w):
        return dot(ctxh[0], w[:H]) + dot(ctxh[1], w[H:])

    other = pl.ds(pl.multiple_of((1 - c) * H, 128), H)
    mixed[:, half] = (strm[:, half].astype(F32) + project(wall[3].reshape(D, H))).astype(BF)
    mixed[:, other] = (strm[:, other].astype(F32) + project(wo_sib[...].reshape(D, H))).astype(BF)
    normed2 = layer_norm(mixed[...].astype(F32), gains[1:2, :]).astype(BF)

    tx[:, :, 0:D] = dot(pick[...], normed2).astype(BF).reshape(NE, R, D)
    tail = dot(pick_x[...], normed2)
    part = lax.div(lax.rem(iota((rows, X), 0), R), 4)
    packed = tail[:, 0:X]
    for p in range(1, 4):
        packed = jnp.where(part == p, tail[:, p * X : (p + 1) * X], packed)
    tx[:, :, D : D + X] = packed.astype(BF).reshape(NE, R, X)

    def in_z(k):
        i = lax.div(k, NX)
        j, odd = lax.div(i, 2), lax.rem(i, 2)
        return (1 - odd) * lax.rem(NZ // 2 - j, NZ // 2) + odd * (NZ // 2 + j)

    def away(k):
        return lax.rem(z + in_z(k), NZ) * NX + lax.rem(x + lax.rem(k, NX), NX)

    def back(k):
        return lax.rem(z + NZ - in_z(k), NZ) * NX + lax.rem(x + NX - lax.rem(k, NX), NX)

    def send_out(k):
        to = away(k)
        return remote(tx.at[to], rx.at[k], t_s.at[k], t_r.at[k], (dp, to))

    def give_back(k, h):
        to = back(k)
        return remote(ry.at[h, k], fx.at[h, ex], f_s.at[h * NE + k], f_r.at[h * NE + k], (dp, to))

    def got_back(k, h):
        src = away(k)
        at = fx.at[h, src]
        return remote(at, at, f_s.at[h * NE + k], f_r.at[h * NE + k], (dp, src))

    @pl.loop(1, NE)
    def _(k):
        send_out(k).start()

    rx[0] = tx[ex]

    r0 = router[...].astype(BF)
    r1 = (router[...] - r0.astype(F32)).astype(BF)
    r2 = (router[...] - r0.astype(F32) - r1.astype(F32)).astype(BF)

    def along(b):
        return lax.dot_general(normed2, b, (((1,), (1,)), ((), ())), preferred_element_type=F32)

    logits = along(r0) + (along(r1) + along(r2))
    expert = iota((F, NE), 1)
    chosen = jnp.concatenate([ids_t[...], jnp.zeros((6, F), jnp.int32)], axis=0).astype(F32).T
    chosen = chosen.astype(jnp.int32)
    first, second = chosen[:, 0:1] == expert, chosen[:, 1:2] == expert
    zero = jnp.zeros_like(logits)
    ahead = jnp.sum(jnp.where(first, logits, zero), axis=1, keepdims=True) - jnp.sum(
        jnp.where(second, logits, zero), axis=1, keepdims=True
    )
    gate = 1.0 / (1.0 + jnp.exp(-ahead))
    gates = jnp.where(first, gate, jnp.where(second, 1.0 - gate, zero))
    either = onehot(first | second)
    earlier = onehot(iota((F, F), 1) < iota((F, F), 0))
    rank_f = jnp.where(first | second, dot(earlier, either), -1.0).astype(BF)
    spread_f = onehot(lax.div(iota((NE, rows), 1), R) == iota((NE, rows), 0))
    rank_f = dot(rank_f, spread_f)
    gates_hi = gates.astype(BF)
    gates_lo = (gates - gates_hi.astype(F32)).astype(BF)
    gates_hi, gates_lo = dot(gates_hi, spread_f), dot(gates_lo, spread_f)
    slot_f = iota((F, rows), 1)

    in_place = rank_f == lax.rem(slot_f, R).astype(F32)
    in_tail = rank_f == (lax.rem(slot_f, 4) + R).astype(F32)

    def on(mask, values):
        return jnp.where(mask, values, 0.0).astype(BF)

    quarter = lax.div(lax.rem(slot_f, R), 4)
    weigh[0] = on(in_place, gates_hi)
    weigh[1] = on(in_place, gates_lo)
    for p in range(4):
        here = in_tail & (quarter == p)
        weigh[2 + 2 * p] = on(here, gates_hi)
        weigh[3 + 2 * p] = on(here, gates_lo)

    chunk_in.relay()
    chunk_out[1].own()

    peers = NE // 2
    whole, more = peers * R, peers * 4
    group = whole + more

    def unpack(p):
        i, j = iota((more, whole), 1), iota((more, whole), 0)
        return onehot(
            (lax.div(i, R) == lax.div(j, 4)) & (lax.rem(i, R) == 4 * p + lax.rem(j, 4))
        )

    def take(g):
        @pl.loop(max(1, g * peers), (g + 1) * peers)
        def _(k):
            at = rx.at[k]
            remote(at, at, t_s.at[k], t_r.at[k], (dp, back(k))).wait_recv()

        mine = slice(g * peers, (g + 1) * peers)
        start = g * group
        xr[start : start + whole] = rx[mine, :, 0:D].reshape(whole, D)
        extra = rx[mine, :, D : D + X].reshape(whole, X)
        for p in range(4):
            xr[start + whole : start + group, p * X : (p + 1) * X] = dot(unpack(p), extra).astype(BF)

    def hide(g, d):
        rows = slice(g * group, (g + 1) * group)
        v = dot(xr[rows], win_all[d])
        hidden[d, rows] = (0.5 * v * (1.0 + jnp.tanh(0.5 * v))).astype(BF)

    def answer(g, h):
        rows = slice(g * group, (g + 1) * group)

        @pl.loop(0, 2 * NY)
        def _(d):
            partial = dot(hidden[d, rows], wout_all[h, d])

            @pl.when(d == 0)
            def _():
                acc[...] = partial

            @pl.when(d > 0)
            def _():
                acc[...] += partial

        mine = slice(g * peers, (g + 1) * peers)
        ry[h, mine, :, 0:H] = acc[0:whole].astype(BF).reshape(peers, R, H)
        packed = None
        for p in range(4):
            piece = lax.dot_general(
                unpack(p),
                acc[whole:group, p * 128 : (p + 1) * 128].astype(BF),
                (((0,), (0,)), ((), ())),
                preferred_element_type=F32,
            )
            packed = piece if packed is None else packed + piece
        ry[h, mine, :, H : H + 128] = packed.astype(BF).reshape(peers, R, 128)

        @pl.loop(max(1, g * peers), (g + 1) * peers)
        def _(k):
            give_back(k, h).start()

        if g == 0:
            fx[h, ex] = ry[h, 0]

    chunk_out[0].relay()
    take(0)
    hide(0, dp)
    chunk_in.from_sib()
    for d in (sib, left, right, of_sib(left), of_sib(right)):
        hide(0, d)
    chunk_in.relay_far()
    chunk_out[1].relay()
    hide(0, far)
    chunk_in.far_from_sib()
    hide(0, of_sib(far))
    chunk_out[0].relay_far()
    take(1)
    for d in (dp, sib, left, right, of_sib(left), of_sib(right), far, of_sib(far)):
        hide(1, d)
    chunk_out[0].from_sib()
    chunk_out[0].far_from_sib()
    answer(0, 0)
    chunk_out[1].relay_far()
    answer(1, 0)
    chunk_out[1].from_sib()
    chunk_out[1].far_from_sib()
    answer(0, 1)
    answer(1, 1)

    for h in range(2):

        @pl.loop(1, NE)
        def _(k):
            got_back(k, h).wait_recv()

        body = fx[h, :, :, 0:H].reshape(rows, H)
        last = fx[h, :, :, H : H + 128].reshape(rows, 128)
        main = dot(weigh[0], body) + dot(weigh[1], body)
        for p in range(4):
            cols = slice(h * H + p * 128, h * H + (p + 1) * 128)
            out[:, cols] = (
                mixed[:, cols].astype(F32)
                + main[:, p * 128 : (p + 1) * 128]
                + (dot(weigh[2 + 2 * p], last) + dot(weigh[3 + 2 * p], last))
            ).astype(BF)

    @pl.loop(1, NE)
    def _(k):
        send_out(k).wait_send()
        give_back(k, 0).wait_send()
        give_back(k, 1).wait_send()

    for copy in sent + [swap, share, give_wo, give_ctx]:
        copy.wait_send()

    def finish(small, large):
        for ring in small + large:
            ring.finish()

    on_core(0, finish)
    on_core(1, finish)


def body(
    frames_in, pit_order, expert_ids, norm_gains, attn_qkv, attn_out, router, expert_in, expert_out
):
    vmem = pl.BlockSpec(memory_space=pltpu.VMEM)
    hbm = pl.BlockSpec(memory_space=pl.ANY)
    dma = pltpu.SemaphoreType.DMA
    rows = NE * R
    out = pl.pallas_call(
        kernel,
        out_shape=jax.ShapeDtypeStruct((F, D), BF),
        in_specs=[vmem] * 5 + [hbm] * 4,
        out_specs=vmem,
        scratch_shapes=[
            pltpu.VMEM((F, D), BF),
            pltpu.VMEM((F, D), BF),
            pltpu.VMEM((2, F, D), BF),
            pltpu.VMEM((4, NZ, NX, D // NE, H), BF),
            pltpu.VMEM((NZ, NX, D // NE, H), BF),
            pltpu.VMEM((3, 2, F, H), BF),
            pltpu.VMEM((2, F, H), BF),
            pltpu.VMEM((F, H), BF),
            pltpu.VMEM((F, D), BF),
            pltpu.VMEM((NE, R, D + X), BF),
            pltpu.VMEM((NE, R, D + X), BF),
            pltpu.VMEM((2, NE, R, H + 128), BF),
            pltpu.VMEM((2, NE, R, H + 128), BF),
            pltpu.VMEM((NE * CAP, D), BF),
            pltpu.VMEM((2 * NY, NE * CAP, H), BF),
            pltpu.VMEM((NE // 2 * CAP, H), F32),
            pltpu.VMEM((2 * NY, D, H), BF),
            pltpu.VMEM((2, 2 * NY, H, H), BF),
            pltpu.VMEM((10, F, rows), BF),
            pltpu.VMEM((rows, F), BF),
            pltpu.VMEM((rows, F), BF),
            dma((48,)),
            dma((48,)),
            dma((27,)),
            dma((27,)),
            dma((4,)),
            dma((4,)),
            dma((NE,)),
            dma((NE,)),
            dma((2 * NE,)),
            dma((2 * NE,)),
            dma((5,)),
        ],
        compiler_params=pltpu.CompilerParams(
            collective_id=0, has_side_effects=True, vmem_limit_bytes=60 * 2**20
        ),
        cost_estimate=pl.CostEstimate(
            flops=14 * 10**9, bytes_accessed=8 * 2**20, transcendentals=4 * 10**6
        ),
    )(
        pit_order.T,
        expert_ids[0].T,
        norm_gains,
        router.T,
        frames_in[0],
        attn_qkv,
        attn_out,
        expert_in[0],
        expert_out[0],
    )
    return out[None]


def solution(mesh):
    return jax.shard_map(
        body,
        mesh=mesh,
        in_specs=(
            P(("dp", "expert"), None, None),
            P(),
            P(("dp", "expert"), None, None),
            P(),
            P(None, "expert", None),
            P("expert", None),
            P(),
            P("expert", None, "dp"),
            P("expert", "dp", None),
        ),
        out_specs=P(("dp", "expert"), None, None),
        check_vma=False,
    )
```

```python
import functools

import jax
import jax.numpy as jnp
from jax import lax
from jax.experimental import pallas as pl
from jax.experimental.pallas import tpu as pltpu
from jax.sharding import PartitionSpec as P

HEAD_DIM = 64
MESH = pl.DeviceIdType.MESH
BF = jnp.bfloat16
F32 = jnp.float32

NX, NZ, NY = 4, 8, 4
NE = NX * NZ
F = 256
D = 1024
H = 512
R = 16
CAP = 20
X = 256
MEETINGS = 128
epsilon = 1e-05


def layer_norm(values, gain):
    mean = jnp.mean(values, axis=-1, keepdims=True)
    centred = values - mean
    spread = jnp.mean(centred * centred, axis=-1, keepdims=True)
    return centred * lax.rsqrt(spread + epsilon) * gain


def dot(a, b):
    return jnp.dot(a, b, preferred_element_type=F32)


def iota(shape, dim):
    return lax.broadcasted_iota(jnp.int32, shape, dim)


def onehot(mask):
    return jnp.where(mask, 1.0, 0.0).astype(BF)


def kernel(
    order,
    ids_t,
    gains,
    router,
    frames,
    qkv,
    wo,
    win,
    wout,
    out,
    pbuf,
    strm,
    normed,
    wall,
    wo_sib,
    proj,
    ctxh,
    ctxs,
    mixed,
    tx,
    rx,
    ry,
    fx,
    xr,
    hidden,
    acc,
    win_all,
    wout_all,
    weigh,
    pick,
    pick_x,
    ring_s,
    ring_r,
    w_s,
    w_r,
    m_s,
    m_r,
    t_s,
    t_r,
    f_s,
    f_r,
    loc,
    line,
):
    dp = lax.axis_index("dp")
    ex = lax.axis_index("expert")
    y, c = lax.div(dp, 2), lax.rem(dp, 2)
    z, x = lax.div(ex, NX), lax.rem(ex, NX)
    sib = y * 2 + (1 - c)

    def at_y(step):
        return lax.rem(y + (step + NY), NY) * 2 + c

    def at_z(step):
        return lax.rem(z + (step + NZ), NZ)

    def at_x(step):
        return lax.rem(x + (step + NX), NX)

    def remote(src, dst, send, recv, to):
        return pltpu.make_async_remote_copy(
            src_ref=src,
            dst_ref=dst,
            send_sem=send,
            recv_sem=recv,
            device_id=to,
            device_id_type=MESH,
        )

    barrier = pltpu.get_barrier_semaphore()

    def greet(to):
        pl.semaphore_signal(barrier, inc=1, device_id=to, device_id_type=MESH)

    for to in (sib, at_y(1), at_y(-1), at_y(2)):
        greet((to, ex))
    for step in range(1, NX):
        greet((dp, z * NX + at_x(step)))
    for step in range(1, NZ):
        greet((dp, at_z(step) * NX + x))

    half = pl.ds(pl.multiple_of(c * H, 128), H)
    mine = [
        pltpu.make_async_copy(qkv.at[:, :, half], wall.at[pl.ds(0, 3), z, x], loc.at[0]),
        pltpu.make_async_copy(wo.at[:, half], wall.at[3, z, x], loc.at[1]),
        pltpu.make_async_copy(win, win_all.at[dp], loc.at[2]),
        pltpu.make_async_copy(wout.at[:, pl.ds(0, H)], wout_all.at[0, dp], loc.at[3]),
        pltpu.make_async_copy(wout.at[:, pl.ds(H, H)], wout_all.at[1, dp], loc.at[4]),
    ]
    for copy in mine:
        copy.start()
    pl.semaphore_wait(barrier, NX - 1 + NZ - 1 + 4)
    for step in range(1, NX):
        pl.semaphore_signal(line, inc=1, device_id=(dp, z * NX + at_x(step)), device_id_type=MESH)

    swap = remote(frames, pbuf, m_s.at[0], m_r.at[0], (at_y(2), ex))
    swap.start()

    class Ring:
        def __init__(self, count, base, view, step_at, device):
            self.last = count // 2
            self.base, self.view, self.step_at, self.device = base, view, step_at, device

        def pair(self, step, hop):
            last = step == self.last
            right = self.view(self.step_at(hop - step), pl.ds(0, H // 2 if last else H))
            left = self.view(self.step_at(step - hop), pl.ds(H // 2 if last else 0, H // 2 if last else H))
            i = self.base + 2 * (step - 1)
            return (
                remote(right, right, ring_s.at[i], ring_r.at[i], self.device(1)),
                remote(left, left, ring_s.at[i + 1], ring_r.at[i + 1], self.device(-1)),
            )

        def begin(self, step):
            for copy in self.pair(step, 1):
                copy.start()

        def wait(self, step):
            for copy in self.pair(step, 0):
                copy.wait_recv()

        def relay(self, step):
            self.wait(step)
            if step < self.last:
                self.begin(step + 1)

        def finish(self):
            for step in range(1, self.last + 1):
                for copy in self.pair(step, 1):
                    copy.wait_send()

    def to_x(step):
        return (dp, z * NX + at_x(step))

    def to_z(step):
        return (dp, at_z(step) * NX + x)

    chunks = ((0, 1), (1, 1), (2, 1), (3, 1))
    small, large = {0: [], 1: []}, {0: [], 1: []}
    for i, (m, n) in enumerate(chunks):
        mats = pl.ds(m, n)
        bx, bz = 12 * i, 12 * i + 4
        small[0].append(Ring(NX, bx, lambda k, w, mats=mats: wall.at[mats, z, k, :, w], at_x, to_x))
        large[0].append(Ring(NZ, bz, lambda k, w, mats=mats: wall.at[mats, k, :, :, w], at_z, to_z))
        small[1].append(Ring(NZ, bz, lambda k, w, mats=mats: wall.at[mats, k, x, :, w], at_z, to_z))
        large[1].append(Ring(NX, bx, lambda k, w, mats=mats: wall.at[mats, :, k, :, w], at_x, to_x))

    mine[0].wait()
    mine[1].wait()

    def on_core(core, work):
        pl.when(c == core)(functools.partial(work, small[core], large[core]))

    def start_small(small, large):
        for ring in small:
            ring.begin(1)

    on_core(0, start_small)
    on_core(1, start_small)

    named = (ids_t[0:1, :] == iota((NE, F), 0)) | (ids_t[1:2, :] == iota((NE, F), 0))
    before = onehot(iota((F, F), 0) < iota((F, F), 1))
    rank = jnp.where(named, dot(onehot(named), before), -1.0).astype(BF)
    rows = NE * R
    spread = onehot(lax.div(iota((rows, NE), 0), R) == iota((rows, NE), 1))
    rank = dot(spread, rank)
    slot = iota((rows, F), 0)
    pick[...] = onehot(rank == lax.rem(slot, R).astype(F32))
    pick_x[...] = onehot(rank == (lax.rem(slot, 4) + R).astype(F32))

    def small_to_large(small, large):
        for step in range(1, small[0].last):
            for ring in small:
                ring.relay(step)
        for near, wide in zip(small, large):
            near.wait(near.last)
            if wide is not large[-1]:
                wide.begin(1)

    on_core(0, small_to_large)
    on_core(1, small_to_large)

    right, left, far = at_y(1), at_y(-1), at_y(2)

    def of_sib(d):
        return d + (1 - 2 * c)

    sent = []

    class Chunk:
        def __init__(self, base, ref, depth):
            self.base, self.ref, self.depth = base, ref, depth

        def copy(self, kind, d, to):
            first = kind in (3, 7)
            rows = pl.ds(0 if first or kind not in (4, 8) else self.depth // 2, self.depth // 2 if kind in (3, 4, 7, 8) else self.depth)
            ref = self.ref.at[d, rows]
            i = self.base + kind
            return remote(ref, ref, w_s.at[i], w_r.at[i], (to, ex))

        def send(self, kind, d, to):
            copy = self.copy(kind, d, to)
            copy.start()
            sent.append(copy)

        def wait(self, kind, d):
            self.copy(kind, d, sib).wait_recv()

        def own(self):
            self.send(0, dp, right)
            self.send(1, dp, left)
            self.send(2, dp, sib)

        def relay(self):
            self.wait(0, left)
            self.send(3, left, right)
            self.send(5, left, sib)
            self.wait(1, right)
            self.send(4, right, left)
            self.send(6, right, sib)

        def relay_far(self):
            self.wait(3, far)
            self.send(7, far, sib)
            self.wait(4, far)
            self.send(8, far, sib)

        def from_sib(self):
            self.wait(2, sib)
            self.wait(5, of_sib(left))
            self.wait(6, of_sib(right))

        def far_from_sib(self):
            self.wait(7, of_sib(far))
            self.wait(8, of_sib(far))

    chunk_in = Chunk(0, win_all, D)
    chunk_out = [Chunk(9 * (1 + h), wout_all.at[h], H) for h in range(2)]
    for copy in mine[2:]:
        copy.wait()
    chunk_in.own()

    def most(small, large):
        steps = large[0].last
        for step in range(1, min(3, steps)):
            for ring in large[:3]:
                ring.relay(step)
            if step == 1:
                large[3].begin(1)
            else:
                large[3].relay(step - 1)

    on_core(0, most)
    on_core(1, most)

    swap.wait_recv()
    speaker = lax.div(y, NY // 2)
    meeting = lax.rem(dp, NY) * NE + ex
    here = (iota((2, MEETINGS), 0) == speaker) & (iota((2, MEETINGS), 1) == meeting)
    source = jnp.sum(jnp.where(here, order[...], 0).astype(F32), axis=(0, 1), keepdims=True)
    stay = source == speaker.astype(F32)
    stream = jnp.where(stay, frames[...].astype(F32), pbuf[...].astype(F32))
    strm[...] = stream.astype(BF)
    normed[c] = layer_norm(stream, gains[0:1, :]).astype(BF)
    share = remote(normed.at[c], normed.at[c], m_s.at[1], m_r.at[1], (sib, ex))
    share.start()

    def rest(small, large):
        for step in range(3, large[0].last):
            for ring in large[:3]:
                ring.relay(step)
            large[3].relay(step - 1)

    def come(m, small, large):
        large[m].wait(large[m].last)

    def output(steps, small, large):
        step = steps[0] if large[3].last == NZ // 2 else steps[1]
        large[3].relay(step)

    def on_both(work):
        on_core(0, work)
        on_core(1, work)

    on_both(rest)
    remote(
        normed.at[1 - c], normed.at[1 - c], m_s.at[1], m_r.at[1], (sib, ex)
    ).wait_recv()
    chunk_out[0].own()

    for m in range(3):
        on_both(functools.partial(come, m))
        w = wall[m].reshape(D, H)
        for s in range(2):
            proj[m, s] = dot(normed[s], w).astype(BF)
        if m == 1:
            on_both(functools.partial(output, (3, 1)))

    lane = iota((F, 128), 1)

    def attend(s, store):
        @pl.loop(0, H // 128)
        def _(h):
            cols = pl.ds(pl.multiple_of(h * 128, 128), 128)
            q = proj[0, s, :, cols] * jnp.asarray(HEAD_DIM**-0.5, BF)
            k = proj[1, s, :, cols]
            v = proj[2, s, :, cols]
            zero = jnp.zeros_like(q)
            for_both = jnp.concatenate(
                [jnp.where(lane < HEAD_DIM, q, zero), jnp.where(lane < HEAD_DIM, zero, q)], axis=0
            )
            scores = lax.dot_general(
                for_both, k, (((1,), (1,)), ((), ())), preferred_element_type=F32
            )
            scores = jnp.exp(scores - jnp.max(scores, axis=-1, keepdims=True))
            probs = (scores / jnp.sum(scores, axis=-1, keepdims=True)).astype(BF)
            both = dot(probs, v)
            store(cols, jnp.where(lane < HEAD_DIM, both[:F], both[F:]).astype(BF))

    def store_other(cols, value):
        ctxs[:, cols] = value

    def store_own(cols, value):
        ctxh[c, :, cols] = value

    attend(1 - c, store_other)
    on_both(functools.partial(output, (4, 2)))
    give_wo = remote(wall.at[3], wo_sib, m_s.at[2], m_r.at[2], (sib, ex))
    give_wo.start()
    give_ctx = remote(ctxs, ctxh.at[c], m_s.at[3], m_r.at[3], (sib, ex))
    give_ctx.start()
    attend(c, store_own)
    remote(wo_sib, wo_sib, m_s.at[2], m_r.at[2], (sib, ex)).wait_recv()
    remote(
        ctxh.at[1 - c], ctxh.at[1 - c], m_s.at[3], m_r.at[3], (sib, ex)
    ).wait_recv()

    def project(w):
        return dot(ctxh[0], w[:H]) + dot(ctxh[1], w[H:])

    other = pl.ds(pl.multiple_of((1 - c) * H, 128), H)
    mixed[:, half] = (strm[:, half].astype(F32) + project(wall[3].reshape(D, H))).astype(BF)
    mixed[:, other] = (strm[:, other].astype(F32) + project(wo_sib[...].reshape(D, H))).astype(BF)
    normed2 = layer_norm(mixed[...].astype(F32), gains[1:2, :]).astype(BF)

    tx[:, :, 0:D] = dot(pick[...], normed2).astype(BF).reshape(NE, R, D)
    tail = dot(pick_x[...], normed2)
    part = lax.div(lax.rem(iota((rows, X), 0), R), 4)
    packed = tail[:, 0:X]
    for p in range(1, 4):
        packed = jnp.where(part == p, tail[:, p * X : (p + 1) * X], packed)
    tx[:, :, D : D + X] = packed.astype(BF).reshape(NE, R, X)

    def in_z(k):
        i = lax.div(k, NX)
        j, odd = lax.div(i, 2), lax.rem(i, 2)
        return (1 - odd) * lax.rem(NZ // 2 - j, NZ // 2) + odd * (NZ // 2 + j)

    def away(k):
        return lax.rem(z + in_z(k), NZ) * NX + lax.rem(x + lax.rem(k, NX), NX)

    def back(k):
        return lax.rem(z + NZ - in_z(k), NZ) * NX + lax.rem(x + NX - lax.rem(k, NX), NX)

    def send_out(k):
        to = away(k)
        return remote(tx.at[to], rx.at[k], t_s.at[0], t_r.at[lax.div(k, NE // 2)], (dp, to))

    def give_back(k, h):
        to = back(k)
        return remote(ry.at[h, k], fx.at[h, ex], f_s.at[h], f_r.at[h], (dp, to))

    def all_of(ref, send, recv):
        return remote(ref, ref, send, recv, (sib, ex))

    pl.semaphore_wait(line, NX - 1)

    @pl.loop(1, NE)
    def _(k):
        send_out(k).start()

    rx[0] = tx[ex]

    chunk_in.relay()

    r0 = router[...].astype(BF)
    r1 = (router[...] - r0.astype(F32)).astype(BF)
    r2 = (router[...] - r0.astype(F32) - r1.astype(F32)).astype(BF)

    def along(b):
        return lax.dot_general(normed2, b, (((1,), (1,)), ((), ())), preferred_element_type=F32)

    logits = along(r0) + (along(r1) + along(r2))
    expert = iota((F, NE), 1)
    chosen = jnp.concatenate([ids_t[...], jnp.zeros((6, F), jnp.int32)], axis=0).astype(F32).T
    chosen = chosen.astype(jnp.int32)
    first, second = chosen[:, 0:1] == expert, chosen[:, 1:2] == expert
    zero = jnp.zeros_like(logits)
    ahead = jnp.sum(jnp.where(first, logits, zero), axis=1, keepdims=True) - jnp.sum(
        jnp.where(second, logits, zero), axis=1, keepdims=True
    )
    gate = 1.0 / (1.0 + jnp.exp(-ahead))
    gates = jnp.where(first, gate, jnp.where(second, 1.0 - gate, zero))
    either = onehot(first | second)
    earlier = onehot(iota((F, F), 1) < iota((F, F), 0))
    rank_f = jnp.where(first | second, dot(earlier, either), -1.0).astype(BF)
    spread_f = onehot(lax.div(iota((NE, rows), 1), R) == iota((NE, rows), 0))
    rank_f = dot(rank_f, spread_f)
    gates_hi = gates.astype(BF)
    gates_lo = (gates - gates_hi.astype(F32)).astype(BF)
    gates_hi, gates_lo = dot(gates_hi, spread_f), dot(gates_lo, spread_f)
    slot_f = iota((F, rows), 1)

    in_place = rank_f == lax.rem(slot_f, R).astype(F32)
    in_tail = rank_f == (lax.rem(slot_f, 4) + R).astype(F32)

    def on(mask, values):
        return jnp.where(mask, values, 0.0).astype(BF)

    quarter = lax.div(lax.rem(slot_f, R), 4)
    weigh[0] = on(in_place, gates_hi)
    weigh[1] = on(in_place, gates_lo)
    for p in range(4):
        here = in_tail & (quarter == p)
        weigh[2 + 2 * p] = on(here, gates_hi)
        weigh[3 + 2 * p] = on(here, gates_lo)


    peers = NE // 2
    whole, more = peers * R, peers * 4
    group = whole + more

    def unpack(p):
        i, j = iota((more, whole), 1), iota((more, whole), 0)
        return onehot(
            (lax.div(i, R) == lax.div(j, 4)) & (lax.rem(i, R) == 4 * p + lax.rem(j, 4))
        )

    def take(g):
        first = max(1, g * peers)
        all_of(rx.at[pl.ds(first, (g + 1) * peers - first)], t_s.at[0], t_r.at[g]).wait_recv()
        mine = slice(g * peers, (g + 1) * peers)
        start = g * group
        xr[start : start + whole] = rx[mine, :, 0:D].reshape(whole, D)
        extra = rx[mine, :, D : D + X].reshape(whole, X)
        for p in range(4):
            xr[start + whole : start + group, p * X : (p + 1) * X] = dot(unpack(p), extra).astype(BF)

    def hide(g, d):
        rows = slice(g * group, (g + 1) * group)
        v = dot(xr[rows], win_all[d])
        hidden[rows, pl.ds(pl.multiple_of(d * H, 128), H)] = (0.5 * v * (1.0 + jnp.tanh(0.5 * v))).astype(BF)

    def answer(g, h):
        rows = slice(g * group, (g + 1) * group)

        acc[...] = dot(hidden[rows], wout_all[h].reshape(2 * NY * H, H))
        mine = slice(g * peers, (g + 1) * peers)
        ry[h, mine, :, 0:H] = acc[0:whole].astype(BF).reshape(peers, R, H)
        packed = None
        for p in range(4):
            piece = lax.dot_general(
                unpack(p),
                acc[whole:group, p * 128 : (p + 1) * 128].astype(BF),
                (((0,), (0,)), ((), ())),
                preferred_element_type=F32,
            )
            packed = piece if packed is None else packed + piece
        ry[h, mine, :, H : H + 128] = packed.astype(BF).reshape(peers, R, 128)

        @pl.loop(max(1, g * peers), (g + 1) * peers)
        def _(k):
            give_back(k, h).start()

        if g == 0:
            fx[h, ex] = ry[h, 0]

    def sent_all():
        for copy in sent + [swap, share, give_wo, give_ctx]:
            copy.wait_send()

        def finish(small, large):
            for ring in small + large:
                ring.finish()

        on_both(finish)
        all_of(tx.at[pl.ds(0, NE - 1)], t_s.at[0], t_r.at[0]).wait_send()

    chunk_out[0].relay()
    chunk_out[1].own()
    take(0)
    hide(0, dp)
    chunk_in.from_sib()
    for d in (sib, left, right, of_sib(left), of_sib(right)):
        hide(0, d)
    chunk_in.relay_far()
    hide(0, far)
    chunk_in.far_from_sib()
    hide(0, of_sib(far))
    chunk_out[0].relay_far()
    chunk_out[0].from_sib()
    chunk_out[0].far_from_sib()
    answer(0, 0)
    take(1)
    for d in (dp, sib, left, right, of_sib(left), of_sib(right), far, of_sib(far)):
        hide(1, d)
    chunk_out[1].relay()
    answer(1, 0)
    chunk_out[1].relay_far()
    chunk_out[1].from_sib()
    chunk_out[1].far_from_sib()
    answer(0, 1)
    answer(1, 1)
    sent_all()

    for h in range(2):

        all_of(fx.at[h, pl.ds(0, NE - 1)], f_s.at[h], f_r.at[h]).wait_recv()
        body = fx[h, :, :, 0:H].reshape(rows, H)
        last = fx[h, :, :, H : H + 128].reshape(rows, 128)
        main = dot(weigh[0], body) + dot(weigh[1], body)
        for p in range(4):
            cols = slice(h * H + p * 128, h * H + (p + 1) * 128)
            out[:, cols] = (
                mixed[:, cols].astype(F32)
                + main[:, p * 128 : (p + 1) * 128]
                + (dot(weigh[2 + 2 * p], last) + dot(weigh[3 + 2 * p], last))
            ).astype(BF)

        all_of(ry.at[h, pl.ds(0, NE - 1)], f_s.at[h], f_r.at[h]).wait_send()


def body(
    frames_in, pit_order, expert_ids, norm_gains, attn_qkv, attn_out, router, expert_in, expert_out
):
    vmem = pl.BlockSpec(memory_space=pltpu.VMEM)
    hbm = pl.BlockSpec(memory_space=pl.ANY)
    dma = pltpu.SemaphoreType.DMA
    rows = NE * R
    out = pl.pallas_call(
        kernel,
        out_shape=jax.ShapeDtypeStruct((F, D), BF),
        in_specs=[vmem] * 5 + [hbm] * 4,
        out_specs=vmem,
        scratch_shapes=[
            pltpu.VMEM((F, D), BF),
            pltpu.VMEM((F, D), BF),
            pltpu.VMEM((2, F, D), BF),
            pltpu.VMEM((4, NZ, NX, D // NE, H), BF),
            pltpu.VMEM((NZ, NX, D // NE, H), BF),
            pltpu.VMEM((3, 2, F, H), BF),
            pltpu.VMEM((2, F, H), BF),
            pltpu.VMEM((F, H), BF),
            pltpu.VMEM((F, D), BF),
            pltpu.VMEM((NE, R, D + X), BF),
            pltpu.VMEM((NE, R, D + X), BF),
            pltpu.VMEM((2, NE, R, H + 128), BF),
            pltpu.VMEM((2, NE, R, H + 128), BF),
            pltpu.VMEM((NE * CAP, D), BF),
            pltpu.VMEM((NE * CAP, 2 * NY * H), BF),
            pltpu.VMEM((NE // 2 * CAP, H), F32),
            pltpu.VMEM((2 * NY, D, H), BF),
            pltpu.VMEM((2, 2 * NY, H, H), BF),
            pltpu.VMEM((10, F, rows), BF),
            pltpu.VMEM((rows, F), BF),
            pltpu.VMEM((rows, F), BF),
            dma((48,)),
            dma((48,)),
            dma((27,)),
            dma((27,)),
            dma((4,)),
            dma((4,)),
            dma((1,)),
            dma((2,)),
            dma((2,)),
            dma((2,)),
            dma((5,)),
            pltpu.SemaphoreType.REGULAR,
        ],
        compiler_params=pltpu.CompilerParams(
            collective_id=0, has_side_effects=True, vmem_limit_bytes=60 * 2**20
        ),
        cost_estimate=pl.CostEstimate(
            flops=14 * 10**9, bytes_accessed=8 * 2**20, transcendentals=4 * 10**6
        ),
    )(
        pit_order.T,
        expert_ids[0].T,
        norm_gains,
        router.T,
        frames_in[0],
        attn_qkv,
        attn_out,
        expert_in[0],
        expert_out[0],
    )
    return out[None]


def solution(mesh):
    return jax.shard_map(
        body,
        mesh=mesh,
        in_specs=(
            P(("dp", "expert"), None, None),
            P(),
            P(("dp", "expert"), None, None),
            P(),
            P(None, "expert", None),
            P("expert", None),
            P(),
            P("expert", None, "dp"),
            P("expert", "dp", None),
        ),
        out_specs=P(("dp", "expert"), None, None),
        check_vma=False,
    )
```

```python
import functools

import jax
import jax.numpy as jnp
from jax import lax
from jax.experimental import pallas as pl
from jax.experimental.pallas import tpu as pltpu
from jax.sharding import PartitionSpec as P

HEAD_DIM = 64
MESH = pl.DeviceIdType.MESH
BF = jnp.bfloat16
F32 = jnp.float32

NX, NZ, NY = 4, 8, 4
NE = NX * NZ
F = 256
D = 1024
H = 512
R = 16
CAP = 20
X = 256
Q = 256
MEETINGS = 128
epsilon = 1e-05


def layer_norm(values, gain):
    mean = jnp.mean(values, axis=-1, keepdims=True)
    centred = values - mean
    spread = jnp.mean(centred * centred, axis=-1, keepdims=True)
    return centred * lax.rsqrt(spread + epsilon) * gain


def dot(a, b):
    return jnp.dot(a, b, preferred_element_type=F32)


def iota(shape, dim):
    return lax.broadcasted_iota(jnp.int32, shape, dim)


def onehot(mask):
    return jnp.where(mask, 1.0, 0.0).astype(BF)


def kernel(
    order,
    ids_t,
    gains,
    router,
    frames,
    qkv,
    wo,
    win,
    wout,
    out,
    pbuf,
    strm,
    normed,
    wall,
    wo_all,
    proj,
    ctxh,
    ctxs,
    mixed,
    tx,
    rx,
    ry0,
    ry1,
    fx0,
    fx1,
    xr,
    hidden,
    acc,
    tail_y,
    win_all,
    wout_all,
    weigh,
    pick,
    pick_x,
    ring_s,
    ring_r,
    w_s,
    w_r,
    m_s,
    m_r,
    t_s,
    t_r,
    f_s,
    f_r,
    loc,
    line,
):
    dp = lax.axis_index("dp")
    ex = lax.axis_index("expert")
    y, c = lax.div(dp, 2), lax.rem(dp, 2)
    z, x = lax.div(ex, NX), lax.rem(ex, NX)
    sib = y * 2 + (1 - c)

    def at_y(step):
        return lax.rem(y + (step + NY), NY) * 2 + c

    def at_z(step):
        return lax.rem(z + (step + NZ), NZ)

    def at_x(step):
        return lax.rem(x + (step + NX), NX)

    def remote(src, dst, send, recv, to):
        return pltpu.make_async_remote_copy(
            src_ref=src,
            dst_ref=dst,
            send_sem=send,
            recv_sem=recv,
            device_id=to,
            device_id_type=MESH,
        )

    barrier = pltpu.get_barrier_semaphore()

    def greet(to):
        pl.semaphore_signal(barrier, inc=1, device_id=to, device_id_type=MESH)

    for to in (sib, at_y(1), at_y(-1), at_y(2)):
        greet((to, ex))
    for step in range(1, NX):
        greet((dp, z * NX + at_x(step)))
    for step in range(1, NZ):
        greet((dp, at_z(step) * NX + x))

    half = pl.ds(pl.multiple_of(c * H, 128), H)
    mine = [
        pltpu.make_async_copy(qkv.at[:, :, half], wall.at[:, z, x], loc.at[0]),
        pltpu.make_async_copy(wo, wo_all.at[z, x], loc.at[1]),
        pltpu.make_async_copy(win, win_all.at[dp], loc.at[2]),
    ] + [
        pltpu.make_async_copy(wout.at[:, pl.ds(q * Q, Q)], wout_all.at[q, dp], loc.at[3 + q])
        for q in range(4)
    ]
    for i, copy in enumerate(mine):
        if i != 1:
            copy.start()

    @pl.when(c == 1)
    def _():
        mine[1].start()

    pl.semaphore_wait(barrier, NX - 1 + NZ - 1 + 4)
    for step in range(1, NX):
        pl.semaphore_signal(line, inc=1, device_id=(dp, z * NX + at_x(step)), device_id_type=MESH)

    swap = remote(frames, pbuf, m_s.at[0], m_r.at[0], (at_y(2), ex))
    swap.start()

    class Ring:
        def __init__(self, count, base, view, step_at, device, width=H):
            self.last, self.width = count // 2, width
            self.base, self.view, self.step_at, self.device = base, view, step_at, device

        def pair(self, step, hop):
            last = step == self.last
            part = self.width // 2 if last else self.width
            right = self.view(self.step_at(hop - step), pl.ds(0, part))
            left = self.view(self.step_at(step - hop), pl.ds(self.width - part, part))
            i = self.base + 2 * (step - 1)
            return (
                remote(right, right, ring_s.at[i], ring_r.at[i], self.device(1)),
                remote(left, left, ring_s.at[i + 1], ring_r.at[i + 1], self.device(-1)),
            )

        def begin(self, step):
            for copy in self.pair(step, 1):
                copy.start()

        def wait(self, step):
            for copy in self.pair(step, 0):
                copy.wait_recv()

        def relay(self, step):
            self.wait(step)
            if step < self.last:
                self.begin(step + 1)

        def finish(self):
            for step in range(1, self.last + 1):
                for copy in self.pair(step, 1):
                    copy.wait_send()

    def to_x(step):
        return (dp, z * NX + at_x(step))

    def to_z(step):
        return (dp, at_z(step) * NX + x)

    small, large = {0: [], 1: []}, {0: [], 1: []}
    for i in range(3):
        mats = i
        bx, bz = 12 * i, 12 * i + 4
        small[0].append(Ring(NX, bx, lambda k, w, mats=mats: wall.at[mats, z, k, :, w], at_x, to_x))
        large[0].append(Ring(NZ, bz, lambda k, w, mats=mats: wall.at[mats, k, :, :, w], at_z, to_z))
        small[1].append(Ring(NZ, bz, lambda k, w, mats=mats: wall.at[mats, k, x, :, w], at_z, to_z))
        large[1].append(Ring(NX, bx, lambda k, w, mats=mats: wall.at[mats, :, k, :, w], at_x, to_x))
    small[1].append(Ring(NZ, 40, lambda k, w: wo_all.at[k, x, :, w], at_z, to_z, D))
    large[1].append(Ring(NX, 36, lambda k, w: wo_all.at[:, k, :, w], at_x, to_x, D))

    mine[0].wait()

    @pl.when(c == 1)
    def _():
        mine[1].wait()


    def on_core(core, work):
        pl.when(c == core)(functools.partial(work, small[core], large[core]))

    def start_small(small, large):
        for ring in small:
            ring.begin(1)

    on_core(0, start_small)
    on_core(1, start_small)

    named = (ids_t[0:1, :] == iota((NE, F), 0)) | (ids_t[1:2, :] == iota((NE, F), 0))
    before = onehot(iota((F, F), 0) < iota((F, F), 1))
    rank = jnp.where(named, dot(onehot(named), before), -1.0).astype(BF)
    rows = NE * R
    spread = onehot(lax.div(iota((rows, NE), 0), R) == iota((rows, NE), 1))
    rank = dot(spread, rank)
    slot = iota((rows, F), 0)
    pick[...] = onehot(rank == lax.rem(slot, R).astype(F32))
    pick_x[...] = onehot(rank == (lax.rem(slot, 4) + R).astype(F32))

    def small_to_large(small, large):
        for step in range(1, small[0].last):
            for ring in small:
                ring.relay(step)
        for near, wide in zip(small, large):
            near.wait(near.last)
            if wide not in large[3:]:
                wide.begin(1)

    on_core(0, small_to_large)
    on_core(1, small_to_large)

    right, left, far = at_y(1), at_y(-1), at_y(2)

    def of_sib(d):
        return d + (1 - 2 * c)

    sent = []

    class Chunk:
        def __init__(self, base, ref, depth):
            self.base, self.ref, self.depth = base, ref, depth

        def copy(self, kind, d, to):
            first = kind in (3, 7)
            rows = pl.ds(0 if first or kind not in (4, 8) else self.depth // 2, self.depth // 2 if kind in (3, 4, 7, 8) else self.depth)
            ref = self.ref.at[d, rows]
            i = self.base + kind
            return remote(ref, ref, w_s.at[i], w_r.at[i], (to, ex))

        def send(self, kind, d, to):
            copy = self.copy(kind, d, to)
            copy.start()
            sent.append(copy)

        def wait(self, kind, d):
            self.copy(kind, d, sib).wait_recv()

        def own(self):
            self.send(0, dp, right)
            self.send(1, dp, left)
            self.send(2, dp, sib)

        def relay(self):
            self.wait(0, left)
            self.send(3, left, right)
            self.send(5, left, sib)
            self.wait(1, right)
            self.send(4, right, left)
            self.send(6, right, sib)

        def relay_far(self):
            self.wait(3, far)
            self.send(7, far, sib)
            self.wait(4, far)
            self.send(8, far, sib)

        def from_sib(self):
            self.wait(2, sib)
            self.wait(5, of_sib(left))
            self.wait(6, of_sib(right))

        def far_from_sib(self):
            self.wait(7, of_sib(far))
            self.wait(8, of_sib(far))

    chunk_in = Chunk(0, win_all, D)
    chunk_out = [Chunk(9 * (1 + q), wout_all.at[q], H) for q in range(4)]
    for copy in mine[2:]:
        copy.wait()
    chunk_in.own()

    def most(small, large):
        steps = large[0].last
        for step in range(1, min(3, steps)):
            for ring in large[:3]:
                ring.relay(step)
            if step == 1 and large[3:]:
                large[3].begin(1)

    on_core(0, most)
    on_core(1, most)

    swap.wait_recv()
    speaker = lax.div(y, NY // 2)
    meeting = lax.rem(dp, NY) * NE + ex
    here = (iota((2, MEETINGS), 0) == speaker) & (iota((2, MEETINGS), 1) == meeting)
    source = jnp.sum(jnp.where(here, order[...], 0).astype(F32), axis=(0, 1), keepdims=True)
    stay = source == speaker.astype(F32)
    stream = jnp.where(stay, frames[...].astype(F32), pbuf[...].astype(F32))
    strm[...] = stream.astype(BF)
    normed[c] = layer_norm(stream, gains[0:1, :]).astype(BF)
    share = remote(normed.at[c], normed.at[c], m_s.at[1], m_r.at[1], (sib, ex))
    share.start()

    def rest(small, large):
        for step in range(3, large[0].last):
            for ring in large[:3]:
                ring.relay(step)

    def come(m, small, large):
        large[m].wait(large[m].last)

    def give_wo(step):
        at = wo_all.at[:, at_x(step)]
        i = 4 + (step + NX) % NX
        return remote(at, at, m_s.at[i], m_r.at[i], (sib, ex))

    def output(small, large):
        large[3].relay(1)
        for step in (0, 1, -1):
            give_wo(step).start()

    def output_end(small, large):
        large[3].wait(2)
        give_wo(2).start()

    def on_both(work):
        on_core(0, work)
        on_core(1, work)

    on_both(rest)
    remote(
        normed.at[1 - c], normed.at[1 - c], m_s.at[1], m_r.at[1], (sib, ex)
    ).wait_recv()
    chunk_out[0].own()

    for m in range(3):
        on_both(functools.partial(come, m))
        w = wall[m].reshape(D, H)
        for s in range(2):
            proj[m, s] = dot(normed[s], w).astype(BF)

    lane = iota((F, 128), 1)

    def attend(s, store):
        @pl.loop(0, H // 128)
        def _(h):
            cols = pl.ds(pl.multiple_of(h * 128, 128), 128)
            q = proj[0, s, :, cols] * jnp.asarray(HEAD_DIM**-0.5, BF)
            k = proj[1, s, :, cols]
            v = proj[2, s, :, cols]
            zero = jnp.zeros_like(q)
            for_both = jnp.concatenate(
                [jnp.where(lane < HEAD_DIM, q, zero), jnp.where(lane < HEAD_DIM, zero, q)], axis=0
            )
            scores = lax.dot_general(
                for_both, k, (((1,), (1,)), ((), ())), preferred_element_type=F32
            )
            scores = jnp.exp(scores - jnp.max(scores, axis=-1, keepdims=True))
            probs = (scores / jnp.sum(scores, axis=-1, keepdims=True)).astype(BF)
            both = dot(probs, v)
            store(cols, jnp.where(lane < HEAD_DIM, both[:F], both[F:]).astype(BF))

    def store_other(cols, value):
        ctxs[:, cols] = value

    def store_own(cols, value):
        ctxh[c, :, cols] = value

    on_core(1, output)
    attend(1 - c, store_other)
    give_ctx = remote(ctxs, ctxh.at[c], m_s.at[3], m_r.at[3], (sib, ex))
    give_ctx.start()
    on_core(1, output_end)
    attend(c, store_own)

    @pl.when(c == 0)
    def _():
        for step in range(NX):
            give_wo(step).wait_recv()

    remote(
        ctxh.at[1 - c], ctxh.at[1 - c], m_s.at[3], m_r.at[3], (sib, ex)
    ).wait_recv()
    w = wo_all[...].reshape(D, D)
    mixed[...] = (strm[...].astype(F32) + (dot(ctxh[0], w[:H]) + dot(ctxh[1], w[H:]))).astype(BF)
    normed2 = layer_norm(mixed[...].astype(F32), gains[1:2, :]).astype(BF)

    tx[:, :, 0:D] = dot(pick[...], normed2).astype(BF).reshape(NE, R, D)
    tail = dot(pick_x[...], normed2)
    part = lax.div(lax.rem(iota((rows, X), 0), R), 4)
    packed = tail[:, 0:X]
    for p in range(1, 4):
        packed = jnp.where(part == p, tail[:, p * X : (p + 1) * X], packed)
    tx[:, :, D : D + X] = packed.astype(BF).reshape(NE, R, X)

    def in_z(k):
        i = lax.div(k, NX)
        j, odd = lax.div(i, 2), lax.rem(i, 2)
        return (1 - odd) * lax.rem(NZ // 2 - j, NZ // 2) + odd * (NZ // 2 + j)

    def away(k):
        return lax.rem(z + in_z(k), NZ) * NX + lax.rem(x + lax.rem(k, NX), NX)

    def back(k):
        return lax.rem(z + NZ - in_z(k), NZ) * NX + lax.rem(x + NX - lax.rem(k, NX), NX)

    def send_out(k):
        to = away(k)
        return remote(tx.at[to], rx.at[k], t_s.at[0], t_r.at[lax.div(k, NE // 2)], (dp, to))

    def quarter_of(even, odd, q):
        return (odd if q % 2 else even).at[q // 2]

    def give_back(k, q):
        to = back(k)
        src, dst = quarter_of(ry0, ry1, q), quarter_of(fx0, fx1, q)
        return remote(src.at[k], dst.at[ex], f_s.at[q], f_r.at[q], (dp, to))

    def all_of(ref, send, recv):
        return remote(ref, ref, send, recv, (sib, ex))

    pl.semaphore_wait(line, NX - 1)

    @pl.loop(1, NE)
    def _(k):
        send_out(k).start()

    rx[0] = tx[ex]

    chunk_in.relay()
    chunk_out[1].own()

    r0 = router[...].astype(BF)
    r1 = (router[...] - r0.astype(F32)).astype(BF)
    r2 = (router[...] - r0.astype(F32) - r1.astype(F32)).astype(BF)

    def along(b):
        return lax.dot_general(normed2, b, (((1,), (1,)), ((), ())), preferred_element_type=F32)

    logits = along(r0) + (along(r1) + along(r2))
    expert = iota((F, NE), 1)
    chosen = jnp.concatenate([ids_t[...], jnp.zeros((6, F), jnp.int32)], axis=0).astype(F32).T
    chosen = chosen.astype(jnp.int32)
    first, second = chosen[:, 0:1] == expert, chosen[:, 1:2] == expert
    zero = jnp.zeros_like(logits)
    ahead = jnp.sum(jnp.where(first, logits, zero), axis=1, keepdims=True) - jnp.sum(
        jnp.where(second, logits, zero), axis=1, keepdims=True
    )
    gate = 1.0 / (1.0 + jnp.exp(-ahead))
    gates = jnp.where(first, gate, jnp.where(second, 1.0 - gate, zero))
    either = onehot(first | second)
    earlier = onehot(iota((F, F), 1) < iota((F, F), 0))
    rank_f = jnp.where(first | second, dot(earlier, either), -1.0).astype(BF)
    spread_f = onehot(lax.div(iota((NE, rows), 1), R) == iota((NE, rows), 0))
    rank_f = dot(rank_f, spread_f)
    gates_hi = gates.astype(BF)
    gates_lo = (gates - gates_hi.astype(F32)).astype(BF)
    gates_hi, gates_lo = dot(gates_hi, spread_f), dot(gates_lo, spread_f)
    slot_f = iota((F, rows), 1)

    in_place = rank_f == lax.rem(slot_f, R).astype(F32)
    in_tail = rank_f == (lax.rem(slot_f, 4) + R).astype(F32)

    def on(mask, values):
        return jnp.where(mask, values, 0.0).astype(BF)

    quarter = lax.div(lax.rem(slot_f, R), 4)
    weigh[0] = on(in_place, gates_hi)
    weigh[1] = on(in_place, gates_lo)
    for p in range(4):
        here = in_tail & (quarter == p)
        weigh[2 + 2 * p] = on(here, gates_hi)
        weigh[3 + 2 * p] = on(here, gates_lo)


    peers = NE // 2
    whole, more = peers * R, peers * 4
    group = whole + more

    def unpack(p):
        i, j = iota((more, whole), 1), iota((more, whole), 0)
        return onehot(
            (lax.div(i, R) == lax.div(j, 4)) & (lax.rem(i, R) == 4 * p + lax.rem(j, 4))
        )

    def take(g):
        first = max(1, g * peers)
        all_of(rx.at[pl.ds(first, (g + 1) * peers - first)], t_s.at[0], t_r.at[g]).wait_recv()
        mine = slice(g * peers, (g + 1) * peers)
        start = g * group
        xr[start : start + whole] = rx[mine, :, 0:D].reshape(whole, D)
        extra = rx[mine, :, D : D + X].reshape(whole, X)
        for p in range(4):
            xr[start + whole : start + group, p * X : (p + 1) * X] = dot(unpack(p), extra).astype(BF)

    def hide(g, d):
        rows = slice(g * group, (g + 1) * group)
        v = dot(xr[rows], win_all[d])
        hidden[rows, pl.ds(pl.multiple_of(d * H, 128), H)] = (0.5 * v * (1.0 + jnp.tanh(0.5 * v))).astype(BF)

    def answer(g, q):
        rows = slice(g * group, (g + 1) * group)
        acc[...] = dot(hidden[rows], wout_all[q].reshape(2 * NY * H, Q)).astype(BF)
        mine = slice(g * peers, (g + 1) * peers)
        ry, fx = quarter_of(ry0, ry1, q), quarter_of(fx0, fx1, q)
        ry[mine, :, 0:Q] = acc[0:whole].reshape(peers, R, Q)
        tail_y[g, :, q % 2 * Q : (q % 2 + 1) * Q] = acc[whole:group]
        if q % 2:
            packed = None
            for p in range(4):
                piece = lax.dot_general(
                    unpack(p),
                    tail_y[g, :, p * 128 : (p + 1) * 128],
                    (((0,), (0,)), ((), ())),
                    preferred_element_type=F32,
                )
                packed = piece if packed is None else packed + piece
            ry[mine, :, Q : Q + 128] = packed.astype(BF).reshape(peers, R, 128)

        @pl.loop(max(1, g * peers), (g + 1) * peers)
        def _(k):
            give_back(k, q).start()

        if g == 0:
            fx[ex] = ry[0]

    def finish_far(chunk):
        chunk.relay_far()
        chunk.from_sib()
        chunk.far_from_sib()

    def sent_all():
        for copy in sent + [swap, share, give_ctx]:
            copy.wait_send()

        def finish(small, large):
            for ring in small + large:
                ring.finish()

        on_both(finish)

        @pl.when(c == 1)
        def _():
            for step in range(NX):
                give_wo(step).wait_send()

        all_of(tx.at[pl.ds(0, NE - 1)], t_s.at[0], t_r.at[0]).wait_send()

    chunk_out[0].relay()
    take(0)
    hide(0, dp)
    chunk_in.from_sib()
    for d in (sib, left, right, of_sib(left), of_sib(right)):
        hide(0, d)
    chunk_in.relay_far()
    hide(0, far)
    chunk_in.far_from_sib()
    hide(0, of_sib(far))
    chunk_out[1].relay()
    chunk_out[2].own()
    chunk_out[3].own()
    finish_far(chunk_out[0])
    answer(0, 0)
    finish_far(chunk_out[1])
    answer(0, 1)
    take(1)
    for d in (dp, sib, left, right, of_sib(left), of_sib(right), far, of_sib(far)):
        hide(1, d)
    chunk_out[2].relay()
    answer(1, 0)
    answer(1, 1)
    chunk_out[3].relay()
    finish_far(chunk_out[2])
    answer(0, 2)
    answer(1, 2)
    finish_far(chunk_out[3])
    answer(0, 3)
    answer(1, 3)
    sent_all()

    def wait_for(q):
        at = quarter_of(fx0, fx1, q).at[pl.ds(0, NE - 1)]
        all_of(at, f_s.at[q], f_r.at[q]).wait_recv()

    for h in range(2):
        main = []
        for q in (2 * h, 2 * h + 1):
            wait_for(q)
            body = quarter_of(fx0, fx1, q)[:, :, 0:Q].reshape(rows, Q)
            main.append(dot(weigh[0], body) + dot(weigh[1], body))
        last = fx1[h, :, :, Q : Q + 128].reshape(rows, 128)
        for p in range(4):
            cols = slice(h * H + p * 128, h * H + (p + 1) * 128)
            out[:, cols] = (
                mixed[:, cols].astype(F32)
                + main[p // 2][:, p % 2 * 128 : (p % 2 + 1) * 128]
                + (dot(weigh[2 + 2 * p], last) + dot(weigh[3 + 2 * p], last))
            ).astype(BF)

    for q in range(4):
        at = quarter_of(ry0, ry1, q).at[pl.ds(0, NE - 1)]
        all_of(at, f_s.at[q], f_r.at[q]).wait_send()


def body(
    frames_in, pit_order, expert_ids, norm_gains, attn_qkv, attn_out, router, expert_in, expert_out
):
    vmem = pl.BlockSpec(memory_space=pltpu.VMEM)
    hbm = pl.BlockSpec(memory_space=pl.ANY)
    dma = pltpu.SemaphoreType.DMA
    rows = NE * R
    out = pl.pallas_call(
        kernel,
        out_shape=jax.ShapeDtypeStruct((F, D), BF),
        in_specs=[vmem] * 5 + [hbm] * 4,
        out_specs=vmem,
        scratch_shapes=[
            pltpu.VMEM((F, D), BF),
            pltpu.VMEM((F, D), BF),
            pltpu.VMEM((2, F, D), BF),
            pltpu.VMEM((3, NZ, NX, D // NE, H), BF),
            pltpu.VMEM((NZ, NX, D // NE, D), BF),
            pltpu.VMEM((3, 2, F, H), BF),
            pltpu.VMEM((2, F, H), BF),
            pltpu.VMEM((F, H), BF),
            pltpu.VMEM((F, D), BF),
            pltpu.VMEM((NE, R, D + X), BF),
            pltpu.VMEM((NE, R, D + X), BF),
            pltpu.VMEM((2, NE, R, Q), BF),
            pltpu.VMEM((2, NE, R, Q + 128), BF),
            pltpu.VMEM((2, NE, R, Q), BF),
            pltpu.VMEM((2, NE, R, Q + 128), BF),
            pltpu.VMEM((NE * CAP, D), BF),
            pltpu.VMEM((NE * CAP, 2 * NY * H), BF),
            pltpu.VMEM((NE // 2 * CAP, Q), BF),
            pltpu.VMEM((2, NE // 2 * 4, H), BF),
            pltpu.VMEM((2 * NY, D, H), BF),
            pltpu.VMEM((4, 2 * NY, H, Q), BF),
            pltpu.VMEM((10, F, rows), BF),
            pltpu.VMEM((rows, F), BF),
            pltpu.VMEM((rows, F), BF),
            dma((48,)),
            dma((48,)),
            dma((45,)),
            dma((45,)),
            dma((8,)),
            dma((8,)),
            dma((1,)),
            dma((2,)),
            dma((4,)),
            dma((4,)),
            dma((7,)),
            pltpu.SemaphoreType.REGULAR,
        ],
        compiler_params=pltpu.CompilerParams(
            collective_id=0, has_side_effects=True, vmem_limit_bytes=60 * 2**20
        ),
        cost_estimate=pl.CostEstimate(
            flops=14 * 10**9, bytes_accessed=8 * 2**20, transcendentals=4 * 10**6
        ),
    )(
        pit_order.T,
        expert_ids[0].T,
        norm_gains,
        router.T,
        frames_in[0],
        attn_qkv,
        attn_out,
        expert_in[0],
        expert_out[0],
    )
    return out[None]


def solution(mesh):
    return jax.shard_map(
        body,
        mesh=mesh,
        in_specs=(
            P(("dp", "expert"), None, None),
            P(),
            P(("dp", "expert"), None, None),
            P(),
            P(None, "expert", None),
            P("expert", None),
            P(),
            P("expert", None, "dp"),
            P("expert", "dp", None),
        ),
        out_specs=P(("dp", "expert"), None, None),
        check_vma=False,
    )
```

```python
import functools

import jax
import jax.numpy as jnp
from jax import lax
from jax.experimental import pallas as pl
from jax.experimental.pallas import tpu as pltpu
from jax.sharding import PartitionSpec as P

HEAD_DIM = 64
MESH = pl.DeviceIdType.MESH
BF = jnp.bfloat16
F32 = jnp.float32

NX, NZ, NY = 4, 8, 4
NE = NX * NZ
F = 256
D = 1024
H = 512
R = 16
CAP = 20
X = 256
Q = 256
MEETINGS = 128
epsilon = 1e-05


def layer_norm(values, gain):
    mean = jnp.mean(values, axis=-1, keepdims=True)
    centred = values - mean
    spread = jnp.mean(centred * centred, axis=-1, keepdims=True)
    return centred * lax.rsqrt(spread + epsilon) * gain


def dot(a, b):
    return jnp.dot(a, b, preferred_element_type=F32)


def iota(shape, dim):
    return lax.broadcasted_iota(jnp.int32, shape, dim)


def onehot(mask):
    return jnp.where(mask, 1.0, 0.0).astype(BF)


def kernel(
    order,
    ids_t,
    gains,
    router,
    frames,
    qkv,
    wo,
    win,
    wout,
    out,
    pbuf,
    strm,
    normed,
    wall,
    wo_sib,
    proj,
    ctxh,
    ctxs,
    mixed,
    tx,
    rx,
    ry0,
    ry1,
    ry2,
    fx0,
    fx1,
    fx2,
    xr,
    hidden,
    acc,
    tail_y,
    win_all,
    wout_a,
    wout_b,
    weigh,
    pick,
    pick_x,
    ring_s,
    ring_r,
    w_s,
    w_r,
    m_s,
    m_r,
    t_s,
    t_r,
    f_s,
    f_r,
    loc,
    line,
):
    dp = lax.axis_index("dp")
    ex = lax.axis_index("expert")
    y, c = lax.div(dp, 2), lax.rem(dp, 2)
    z, x = lax.div(ex, NX), lax.rem(ex, NX)
    sib = y * 2 + (1 - c)

    def at_y(step):
        return lax.rem(y + (step + NY), NY) * 2 + c

    def at_z(step):
        return lax.rem(z + (step + NZ), NZ)

    def at_x(step):
        return lax.rem(x + (step + NX), NX)

    def remote(src, dst, send, recv, to):
        return pltpu.make_async_remote_copy(
            src_ref=src,
            dst_ref=dst,
            send_sem=send,
            recv_sem=recv,
            device_id=to,
            device_id_type=MESH,
        )

    barrier = pltpu.get_barrier_semaphore()

    def greet(to):
        pl.semaphore_signal(barrier, inc=1, device_id=to, device_id_type=MESH)

    for to in (sib, at_y(1), at_y(-1), at_y(2)):
        greet((to, ex))
    for step in range(1, NX):
        greet((dp, z * NX + at_x(step)))
    for step in range(1, NZ):
        greet((dp, at_z(step) * NX + x))

    half = pl.ds(pl.multiple_of(c * H, 128), H)
    mine = [
        pltpu.make_async_copy(qkv.at[:, :, half], wall.at[pl.ds(0, 3), z, x], loc.at[0]),
        pltpu.make_async_copy(wo.at[:, half], wall.at[3, z, x], loc.at[1]),
        pltpu.make_async_copy(win, win_all.at[dp], loc.at[2]),
        pltpu.make_async_copy(wout.at[:, pl.ds(0, H)], wout_a.at[dp], loc.at[3]),
        pltpu.make_async_copy(wout.at[:, pl.ds(H, Q)], wout_b.at[0, dp], loc.at[4]),
        pltpu.make_async_copy(wout.at[:, pl.ds(H + Q, Q)], wout_b.at[1, dp], loc.at[5]),
    ]
    for copy in mine:
        copy.start()
    pl.semaphore_wait(barrier, NX - 1 + NZ - 1 + 4)
    for step in range(1, NX):
        pl.semaphore_signal(line, inc=1, device_id=(dp, z * NX + at_x(step)), device_id_type=MESH)

    swap = remote(frames, pbuf, m_s.at[0], m_r.at[0], (at_y(2), ex))
    swap.start()

    class Ring:
        def __init__(self, count, base, view, step_at, device):
            self.last = count // 2
            self.base, self.view, self.step_at, self.device = base, view, step_at, device

        def pair(self, step, hop):
            last = step == self.last
            right = self.view(self.step_at(hop - step), pl.ds(0, H // 2 if last else H))
            left = self.view(self.step_at(step - hop), pl.ds(H // 2 if last else 0, H // 2 if last else H))
            i = self.base + 2 * (step - 1)
            return (
                remote(right, right, ring_s.at[i], ring_r.at[i], self.device(1)),
                remote(left, left, ring_s.at[i + 1], ring_r.at[i + 1], self.device(-1)),
            )

        def begin(self, step):
            for copy in self.pair(step, 1):
                copy.start()

        def wait(self, step):
            for copy in self.pair(step, 0):
                copy.wait_recv()

        def relay(self, step):
            self.wait(step)
            if step < self.last:
                self.begin(step + 1)

        def finish(self):
            for step in range(1, self.last + 1):
                for copy in self.pair(step, 1):
                    copy.wait_send()

    def to_x(step):
        return (dp, z * NX + at_x(step))

    def to_z(step):
        return (dp, at_z(step) * NX + x)

    chunks = ((0, 1), (1, 1), (2, 1), (3, 1))
    small, large = {0: [], 1: []}, {0: [], 1: []}
    for i, (m, n) in enumerate(chunks):
        mats = pl.ds(m, n)
        bx, bz = 12 * i, 12 * i + 4
        small[0].append(Ring(NX, bx, lambda k, w, mats=mats: wall.at[mats, z, k, :, w], at_x, to_x))
        large[0].append(Ring(NZ, bz, lambda k, w, mats=mats: wall.at[mats, k, :, :, w], at_z, to_z))
        small[1].append(Ring(NZ, bz, lambda k, w, mats=mats: wall.at[mats, k, x, :, w], at_z, to_z))
        large[1].append(Ring(NX, bx, lambda k, w, mats=mats: wall.at[mats, :, k, :, w], at_x, to_x))

    mine[0].wait()
    mine[1].wait()

    def on_core(core, work):
        pl.when(c == core)(functools.partial(work, small[core], large[core]))

    def start_small(small, large):
        for ring in small:
            ring.begin(1)

    on_core(0, start_small)
    on_core(1, start_small)

    named = (ids_t[0:1, :] == iota((NE, F), 0)) | (ids_t[1:2, :] == iota((NE, F), 0))
    before = onehot(iota((F, F), 0) < iota((F, F), 1))
    rank = jnp.where(named, dot(onehot(named), before), -1.0).astype(BF)
    rows = NE * R
    spread = onehot(lax.div(iota((rows, NE), 0), R) == iota((rows, NE), 1))
    rank = dot(spread, rank)
    slot = iota((rows, F), 0)
    pick[...] = onehot(rank == lax.rem(slot, R).astype(F32))
    pick_x[...] = onehot(rank == (lax.rem(slot, 4) + R).astype(F32))

    def small_to_large(small, large):
        for step in range(1, small[0].last):
            for ring in small:
                ring.relay(step)
        for near, wide in zip(small, large):
            near.wait(near.last)
            if wide is not large[-1]:
                wide.begin(1)


    right, left, far = at_y(1), at_y(-1), at_y(2)

    def of_sib(d):
        return d + (1 - 2 * c)

    sent = []

    class Chunk:
        def __init__(self, base, ref, depth):
            self.base, self.ref, self.depth = base, ref, depth

        def copy(self, kind, d, to):
            first = kind in (3, 7)
            rows = pl.ds(0 if first or kind not in (4, 8) else self.depth // 2, self.depth // 2 if kind in (3, 4, 7, 8) else self.depth)
            ref = self.ref.at[d, rows]
            i = self.base + kind
            return remote(ref, ref, w_s.at[i], w_r.at[i], (to, ex))

        def send(self, kind, d, to):
            copy = self.copy(kind, d, to)
            copy.start()
            sent.append(copy)

        def wait(self, kind, d):
            self.copy(kind, d, sib).wait_recv()

        def own(self):
            self.send(0, dp, right)
            self.send(1, dp, left)
            self.send(2, dp, sib)

        def relay(self):
            self.wait(0, left)
            self.send(3, left, right)
            self.send(5, left, sib)
            self.wait(1, right)
            self.send(4, right, left)
            self.send(6, right, sib)

        def relay_far(self):
            self.wait(3, far)
            self.send(7, far, sib)
            self.wait(4, far)
            self.send(8, far, sib)

        def from_sib(self):
            self.wait(2, sib)
            self.wait(5, of_sib(left))
            self.wait(6, of_sib(right))

        def far_from_sib(self):
            self.wait(7, of_sib(far))
            self.wait(8, of_sib(far))

    chunk_in = Chunk(0, win_all, D)
    chunk_out = [Chunk(9, wout_a, H), Chunk(18, wout_b.at[0], H), Chunk(27, wout_b.at[1], H)]
    for copy in mine[2:]:
        copy.wait()
    chunk_in.own()
    on_core(0, small_to_large)
    on_core(1, small_to_large)

    def most(small, large):
        steps = large[0].last
        for step in range(1, min(3, steps)):
            for ring in large[:3]:
                ring.relay(step)
            if step == 1:
                large[3].begin(1)
            else:
                large[3].relay(step - 1)

    on_core(0, most)
    on_core(1, most)

    swap.wait_recv()
    speaker = lax.div(y, NY // 2)
    meeting = lax.rem(dp, NY) * NE + ex
    here = (iota((2, MEETINGS), 0) == speaker) & (iota((2, MEETINGS), 1) == meeting)
    source = jnp.sum(jnp.where(here, order[...], 0).astype(F32), axis=(0, 1), keepdims=True)
    stay = source == speaker.astype(F32)
    stream = jnp.where(stay, frames[...].astype(F32), pbuf[...].astype(F32))
    strm[...] = stream.astype(BF)
    normed[c] = layer_norm(stream, gains[0:1, :]).astype(BF)
    share = remote(normed.at[c], normed.at[c], m_s.at[1], m_r.at[1], (sib, ex))
    share.start()

    def rest(small, large):
        for step in range(3, large[0].last):
            for ring in large[:3]:
                ring.relay(step)
            large[3].relay(step - 1)

    def come(m, small, large):
        large[m].wait(large[m].last)

    def output(steps, small, large):
        step = steps[0] if large[3].last == NZ // 2 else steps[1]
        large[3].relay(step)

    def on_both(work):
        on_core(0, work)
        on_core(1, work)

    on_both(rest)
    remote(
        normed.at[1 - c], normed.at[1 - c], m_s.at[1], m_r.at[1], (sib, ex)
    ).wait_recv()
    chunk_out[0].own()

    for m in range(3):
        on_both(functools.partial(come, m))
        w = wall[m].reshape(D, H)
        for s in range(2):
            proj[m, s] = dot(normed[s], w).astype(BF)
        if m == 1:
            on_both(functools.partial(output, (3, 1)))

    lane = iota((F, 128), 1)

    def attend(s, store):
        @pl.loop(0, H // 128)
        def _(h):
            cols = pl.ds(pl.multiple_of(h * 128, 128), 128)
            q = proj[0, s, :, cols] * jnp.asarray(HEAD_DIM**-0.5, BF)
            k = proj[1, s, :, cols]
            v = proj[2, s, :, cols]
            zero = jnp.zeros_like(q)
            for_both = jnp.concatenate(
                [jnp.where(lane < HEAD_DIM, q, zero), jnp.where(lane < HEAD_DIM, zero, q)], axis=0
            )
            scores = lax.dot_general(
                for_both, k, (((1,), (1,)), ((), ())), preferred_element_type=F32
            )
            scores = jnp.exp(scores - jnp.max(scores, axis=-1, keepdims=True))
            probs = (scores / jnp.sum(scores, axis=-1, keepdims=True)).astype(BF)
            both = dot(probs, v)
            store(cols, jnp.where(lane < HEAD_DIM, both[:F], both[F:]).astype(BF))

    def store_other(cols, value):
        ctxs[:, cols] = value

    def store_own(cols, value):
        ctxh[c, :, cols] = value

    attend(1 - c, store_other)
    on_both(functools.partial(output, (4, 2)))
    give_wo = remote(wall.at[3], wo_sib, m_s.at[2], m_r.at[2], (sib, ex))
    give_wo.start()
    give_ctx = remote(ctxs, ctxh.at[c], m_s.at[3], m_r.at[3], (sib, ex))
    give_ctx.start()
    attend(c, store_own)
    remote(wo_sib, wo_sib, m_s.at[2], m_r.at[2], (sib, ex)).wait_recv()
    remote(
        ctxh.at[1 - c], ctxh.at[1 - c], m_s.at[3], m_r.at[3], (sib, ex)
    ).wait_recv()

    def project(w):
        return dot(ctxh[0], w[:H]) + dot(ctxh[1], w[H:])

    other = pl.ds(pl.multiple_of((1 - c) * H, 128), H)
    mixed[:, half] = (strm[:, half].astype(F32) + project(wall[3].reshape(D, H))).astype(BF)
    mixed[:, other] = (strm[:, other].astype(F32) + project(wo_sib[...].reshape(D, H))).astype(BF)
    normed2 = layer_norm(mixed[...].astype(F32), gains[1:2, :]).astype(BF)

    tx[:, :, 0:D] = dot(pick[...], normed2).astype(BF).reshape(NE, R, D)
    tail = dot(pick_x[...], normed2)
    part = lax.div(lax.rem(iota((rows, X), 0), R), 4)
    packed = tail[:, 0:X]
    for p in range(1, 4):
        packed = jnp.where(part == p, tail[:, p * X : (p + 1) * X], packed)
    tx[:, :, D : D + X] = packed.astype(BF).reshape(NE, R, X)

    def in_z(k):
        i = lax.div(k, NX)
        j, odd = lax.div(i, 2), lax.rem(i, 2)
        return (1 - odd) * lax.rem(NZ // 2 - j, NZ // 2) + odd * (NZ // 2 + j)

    def away(k):
        return lax.rem(z + in_z(k), NZ) * NX + lax.rem(x + lax.rem(k, NX), NX)

    def back(k):
        return lax.rem(z + NZ - in_z(k), NZ) * NX + lax.rem(x + NX - lax.rem(k, NX), NX)

    def send_out(k):
        to = away(k)
        return remote(tx.at[to], rx.at[k], t_s.at[0], t_r.at[lax.div(k, NE // 2)], (dp, to))

    ry, fx = (ry0, ry1, ry2), (fx0, fx1, fx2)

    def give_back(k, q):
        to = back(k)
        return remote(ry[q].at[k], fx[q].at[ex], f_s.at[q], f_r.at[q], (dp, to))

    def all_of(ref, send, recv):
        return remote(ref, ref, send, recv, (sib, ex))

    pl.semaphore_wait(line, NX - 1)

    @pl.loop(1, NE)
    def _(k):
        send_out(k).start()

    rx[0] = tx[ex]

    chunk_in.relay()

    r0 = router[...].astype(BF)
    r1 = (router[...] - r0.astype(F32)).astype(BF)
    r2 = (router[...] - r0.astype(F32) - r1.astype(F32)).astype(BF)

    def along(b):
        return lax.dot_general(normed2, b, (((1,), (1,)), ((), ())), preferred_element_type=F32)

    logits = along(r0) + (along(r1) + along(r2))
    expert = iota((F, NE), 1)
    chosen = jnp.concatenate([ids_t[...], jnp.zeros((6, F), jnp.int32)], axis=0).astype(F32).T
    chosen = chosen.astype(jnp.int32)
    first, second = chosen[:, 0:1] == expert, chosen[:, 1:2] == expert
    zero = jnp.zeros_like(logits)
    ahead = jnp.sum(jnp.where(first, logits, zero), axis=1, keepdims=True) - jnp.sum(
        jnp.where(second, logits, zero), axis=1, keepdims=True
    )
    gate = 1.0 / (1.0 + jnp.exp(-ahead))
    gates = jnp.where(first, gate, jnp.where(second, 1.0 - gate, zero))
    either = onehot(first | second)
    earlier = onehot(iota((F, F), 1) < iota((F, F), 0))
    rank_f = jnp.where(first | second, dot(earlier, either), -1.0).astype(BF)
    spread_f = onehot(lax.div(iota((NE, rows), 1), R) == iota((NE, rows), 0))
    rank_f = dot(rank_f, spread_f)
    gates_hi = gates.astype(BF)
    gates_lo = (gates - gates_hi.astype(F32)).astype(BF)
    gates_hi, gates_lo = dot(gates_hi, spread_f), dot(gates_lo, spread_f)
    slot_f = iota((F, rows), 1)

    in_place = rank_f == lax.rem(slot_f, R).astype(F32)
    in_tail = rank_f == (lax.rem(slot_f, 4) + R).astype(F32)

    def on(mask, values):
        return jnp.where(mask, values, 0.0).astype(BF)

    quarter = lax.div(lax.rem(slot_f, R), 4)
    weigh[0] = on(in_place, gates_hi)
    weigh[1] = on(in_place, gates_lo)
    for p in range(4):
        here = in_tail & (quarter == p)
        weigh[2 + 2 * p] = on(here, gates_hi)
        weigh[3 + 2 * p] = on(here, gates_lo)


    peers = NE // 2
    whole, more = peers * R, peers * 4
    group = whole + more

    def unpack(p):
        i, j = iota((more, whole), 1), iota((more, whole), 0)
        return onehot(
            (lax.div(i, R) == lax.div(j, 4)) & (lax.rem(i, R) == 4 * p + lax.rem(j, 4))
        )

    def take(g):
        first = max(1, g * peers)
        all_of(rx.at[pl.ds(first, (g + 1) * peers - first)], t_s.at[0], t_r.at[g]).wait_recv()
        mine = slice(g * peers, (g + 1) * peers)
        start = g * group
        xr[start : start + whole] = rx[mine, :, 0:D].reshape(whole, D)
        extra = rx[mine, :, D : D + X].reshape(whole, X)
        for p in range(4):
            xr[start + whole : start + group, p * X : (p + 1) * X] = dot(unpack(p), extra).astype(BF)

    def hide(g, d):
        rows = slice(g * group, (g + 1) * group)
        v = dot(xr[rows], win_all[d])
        hidden[rows, pl.ds(pl.multiple_of(d * H, 128), H)] = (0.5 * v * (1.0 + jnp.tanh(0.5 * v))).astype(BF)

    def answer(g, q):
        rows = slice(g * group, (g + 1) * group)
        mine = slice(g * peers, (g + 1) * peers)
        wide = H if q == 0 else Q
        w = wout_a[...] if q == 0 else wout_b[q - 1]
        acc[:, 0:wide] = dot(hidden[rows], w.reshape(2 * NY * H, wide)).astype(BF)
        ry[q][mine, :, 0:wide] = acc[0:whole, 0:wide].reshape(peers, R, wide)
        start = Q if q == 2 else 0
        tail_y[g, :, start : start + wide] = acc[whole:group, 0:wide]
        if q != 1:
            packed = None
            for p in range(4):
                piece = lax.dot_general(
                    unpack(p),
                    tail_y[g, :, p * 128 : (p + 1) * 128],
                    (((0,), (0,)), ((), ())),
                    preferred_element_type=F32,
                )
                packed = piece if packed is None else packed + piece
            ry[q][mine, :, wide : wide + 128] = packed.astype(BF).reshape(peers, R, 128)

        @pl.loop(max(1, g * peers), (g + 1) * peers)
        def _(k):
            give_back(k, q).start()

        if g == 0:
            fx[q][ex] = ry[q][0]

    def finish_far(chunk):
        chunk.relay_far()
        chunk.from_sib()
        chunk.far_from_sib()

    def sent_all():
        for copy in sent + [swap, share, give_wo, give_ctx]:
            copy.wait_send()

        def finish(small, large):
            for ring in small + large:
                ring.finish()

        on_both(finish)
        all_of(tx.at[pl.ds(0, NE - 1)], t_s.at[0], t_r.at[0]).wait_send()

    chunk_out[0].relay()
    chunk_out[1].own()
    chunk_out[2].own()
    take(0)
    hide(0, dp)
    chunk_in.from_sib()
    for d in (sib, left, right, of_sib(left), of_sib(right)):
        hide(0, d)
    chunk_in.relay_far()
    hide(0, far)
    chunk_in.far_from_sib()
    hide(0, of_sib(far))
    finish_far(chunk_out[0])
    answer(0, 0)
    take(1)
    chunk_out[1].relay()
    for d in (dp, sib, left, right, of_sib(left), of_sib(right), far, of_sib(far)):
        hide(1, d)
    chunk_out[2].relay()
    answer(1, 0)
    finish_far(chunk_out[1])
    answer(0, 1)
    answer(1, 1)
    finish_far(chunk_out[2])
    answer(0, 2)
    answer(1, 2)
    sent_all()

    def wait_for(q):
        all_of(fx[q].at[pl.ds(0, NE - 1)], f_s.at[q], f_r.at[q]).wait_recv()
        wide = H if q == 0 else Q
        body = fx[q][:, :, 0:wide].reshape(rows, wide)
        return dot(weigh[0], body) + dot(weigh[1], body)

    def combine(start, main, last):
        for p in range(4):
            cols = slice(start + p * 128, start + (p + 1) * 128)
            i = 0 if len(main) == 1 else p // 2
            at = (p if len(main) == 1 else p % 2) * 128
            out[:, cols] = (
                mixed[:, cols].astype(F32)
                + main[i][:, at : at + 128]
                + (dot(weigh[2 + 2 * p], last) + dot(weigh[3 + 2 * p], last))
            ).astype(BF)

    main = [wait_for(0)]
    combine(0, main, fx0[:, :, H : H + 128].reshape(rows, 128))
    main = [wait_for(1), wait_for(2)]
    combine(H, main, fx2[:, :, Q : Q + 128].reshape(rows, 128))
    for q in range(3):
        all_of(ry[q].at[pl.ds(0, NE - 1)], f_s.at[q], f_r.at[q]).wait_send()


def body(
    frames_in, pit_order, expert_ids, norm_gains, attn_qkv, attn_out, router, expert_in, expert_out
):
    vmem = pl.BlockSpec(memory_space=pltpu.VMEM)
    hbm = pl.BlockSpec(memory_space=pl.ANY)
    dma = pltpu.SemaphoreType.DMA
    rows = NE * R
    out = pl.pallas_call(
        kernel,
        out_shape=jax.ShapeDtypeStruct((F, D), BF),
        in_specs=[vmem] * 5 + [hbm] * 4,
        out_specs=vmem,
        scratch_shapes=[
            pltpu.VMEM((F, D), BF),
            pltpu.VMEM((F, D), BF),
            pltpu.VMEM((2, F, D), BF),
            pltpu.VMEM((4, NZ, NX, D // NE, H), BF),
            pltpu.VMEM((NZ, NX, D // NE, H), BF),
            pltpu.VMEM((3, 2, F, H), BF),
            pltpu.VMEM((2, F, H), BF),
            pltpu.VMEM((F, H), BF),
            pltpu.VMEM((F, D), BF),
            pltpu.VMEM((NE, R, D + X), BF),
            pltpu.VMEM((NE, R, D + X), BF),
            pltpu.VMEM((NE, R, H + 128), BF),
            pltpu.VMEM((NE, R, Q), BF),
            pltpu.VMEM((NE, R, Q + 128), BF),
            pltpu.VMEM((NE, R, H + 128), BF),
            pltpu.VMEM((NE, R, Q), BF),
            pltpu.VMEM((NE, R, Q + 128), BF),
            pltpu.VMEM((NE * CAP, D), BF),
            pltpu.VMEM((NE * CAP, 2 * NY * H), BF),
            pltpu.VMEM((NE // 2 * CAP, H), BF),
            pltpu.VMEM((2, NE // 2 * 4, H), BF),
            pltpu.VMEM((2 * NY, D, H), BF),
            pltpu.VMEM((2 * NY, H, H), BF),
            pltpu.VMEM((2, 2 * NY, H, Q), BF),
            pltpu.VMEM((10, F, rows), BF),
            pltpu.VMEM((rows, F), BF),
            pltpu.VMEM((rows, F), BF),
            dma((48,)),
            dma((48,)),
            dma((36,)),
            dma((36,)),
            dma((4,)),
            dma((4,)),
            dma((1,)),
            dma((2,)),
            dma((3,)),
            dma((3,)),
            dma((6,)),
            pltpu.SemaphoreType.REGULAR,
        ],
        compiler_params=pltpu.CompilerParams(
            collective_id=0, has_side_effects=True, vmem_limit_bytes=60 * 2**20
        ),
        cost_estimate=pl.CostEstimate(
            flops=14 * 10**9, bytes_accessed=8 * 2**20, transcendentals=4 * 10**6
        ),
    )(
        pit_order.T,
        expert_ids[0].T,
        norm_gains,
        router.T,
        frames_in[0],
        attn_qkv,
        attn_out,
        expert_in[0],
        expert_out[0],
    )
    return out[None]


def solution(mesh):
    return jax.shard_map(
        body,
        mesh=mesh,
        in_specs=(
            P(("dp", "expert"), None, None),
            P(),
            P(("dp", "expert"), None, None),
            P(),
            P(None, "expert", None),
            P("expert", None),
            P(),
            P("expert", None, "dp"),
            P("expert", "dp", None),
        ),
        out_specs=P(("dp", "expert"), None, None),
        check_vma=False,
    )
```

```python
import functools

import jax
import jax.numpy as jnp
from jax import lax
from jax.experimental import pallas as pl
from jax.experimental.pallas import tpu as pltpu
from jax.sharding import PartitionSpec as P

HEAD_DIM = 64
MESH = pl.DeviceIdType.MESH
BF = jnp.bfloat16
F32 = jnp.float32

NX, NZ, NY = 4, 8, 4
NE = NX * NZ
F = 256
D = 1024
H = 512
R = 16
CAP = 20
X = 256
Q = 256
MEETINGS = 128
epsilon = 1e-05


def layer_norm(values, gain):
    mean = jnp.mean(values, axis=-1, keepdims=True)
    centred = values - mean
    spread = jnp.mean(centred * centred, axis=-1, keepdims=True)
    return centred * lax.rsqrt(spread + epsilon) * gain


def dot(a, b):
    return jnp.dot(a, b, preferred_element_type=F32)


def iota(shape, dim):
    return lax.broadcasted_iota(jnp.int32, shape, dim)


def onehot(mask):
    return jnp.where(mask, 1.0, 0.0).astype(BF)


def kernel(
    order,
    ids_t,
    gains,
    router,
    frames,
    qkv,
    wo,
    win,
    wout,
    out,
    pbuf,
    strm,
    normed,
    wall,
    wo_sib,
    proj,
    ctxh,
    ctxs,
    mixed,
    tx,
    rx,
    ry0,
    ry1,
    ry2,
    fx0,
    fx1,
    fx2,
    xr,
    hidden,
    acc,
    tail_y,
    win_all,
    wout_a,
    wout_b,
    weigh,
    pick,
    pick_x,
    ring_s,
    ring_r,
    w_s,
    w_r,
    m_s,
    m_r,
    t_s,
    t_r,
    f_s,
    f_r,
    loc,
    line,
):
    dp = lax.axis_index("dp")
    ex = lax.axis_index("expert")
    y, c = lax.div(dp, 2), lax.rem(dp, 2)
    z, x = lax.div(ex, NX), lax.rem(ex, NX)
    sib = y * 2 + (1 - c)

    def at_y(step):
        return lax.rem(y + (step + NY), NY) * 2 + c

    def at_z(step):
        return lax.rem(z + (step + NZ), NZ)

    def at_x(step):
        return lax.rem(x + (step + NX), NX)

    def remote(src, dst, send, recv, to):
        return pltpu.make_async_remote_copy(
            src_ref=src,
            dst_ref=dst,
            send_sem=send,
            recv_sem=recv,
            device_id=to,
            device_id_type=MESH,
        )

    barrier = pltpu.get_barrier_semaphore()

    def greet(to):
        pl.semaphore_signal(barrier, inc=1, device_id=to, device_id_type=MESH)

    for to in (sib, at_y(1), at_y(-1), at_y(2)):
        greet((to, ex))
    for step in range(1, NX):
        greet((dp, z * NX + at_x(step)))
    for step in range(1, NZ):
        greet((dp, at_z(step) * NX + x))

    half = pl.ds(pl.multiple_of(c * H, 128), H)
    mine = [
        pltpu.make_async_copy(qkv.at[:, :, half], wall.at[pl.ds(0, 3), z, x], loc.at[0]),
        pltpu.make_async_copy(wo.at[:, half], wall.at[3, z, x], loc.at[1]),
        pltpu.make_async_copy(win, win_all.at[dp], loc.at[2]),
        pltpu.make_async_copy(wout.at[:, pl.ds(0, H)], wout_a.at[dp], loc.at[3]),
        pltpu.make_async_copy(wout.at[:, pl.ds(H, Q)], wout_b.at[0, dp], loc.at[4]),
        pltpu.make_async_copy(wout.at[:, pl.ds(H + Q, Q)], wout_b.at[1, dp], loc.at[5]),
    ]
    for copy in mine:
        copy.start()
    pl.semaphore_wait(barrier, NX - 1 + NZ - 1 + 4)
    for step in range(1, NX):
        pl.semaphore_signal(line, inc=1, device_id=(dp, z * NX + at_x(step)), device_id_type=MESH)

    swap = remote(frames, pbuf, m_s.at[0], m_r.at[0], (at_y(2), ex))
    swap.start()

    class Ring:
        def __init__(self, count, base, view, step_at, device):
            self.last = count // 2
            self.base, self.view, self.step_at, self.device = base, view, step_at, device

        def pair(self, step, hop):
            last = step == self.last
            right = self.view(self.step_at(hop - step), pl.ds(0, H // 2 if last else H))
            left = self.view(self.step_at(step - hop), pl.ds(H // 2 if last else 0, H // 2 if last else H))
            i = self.base + 2 * (step - 1)
            return (
                remote(right, right, ring_s.at[i], ring_r.at[i], self.device(1)),
                remote(left, left, ring_s.at[i + 1], ring_r.at[i + 1], self.device(-1)),
            )

        def begin(self, step):
            for copy in self.pair(step, 1):
                copy.start()

        def wait(self, step):
            for copy in self.pair(step, 0):
                copy.wait_recv()

        def relay(self, step):
            self.wait(step)
            if step < self.last:
                self.begin(step + 1)

        def finish(self):
            for step in range(1, self.last + 1):
                for copy in self.pair(step, 1):
                    copy.wait_send()

    def to_x(step):
        return (dp, z * NX + at_x(step))

    def to_z(step):
        return (dp, at_z(step) * NX + x)

    chunks = ((0, 1), (1, 1), (2, 1), (3, 1))
    small, large = {0: [], 1: []}, {0: [], 1: []}
    for i, (m, n) in enumerate(chunks):
        mats = pl.ds(m, n)
        bx, bz = 12 * i, 12 * i + 4
        small[0].append(Ring(NX, bx, lambda k, w, mats=mats: wall.at[mats, z, k, :, w], at_x, to_x))
        large[0].append(Ring(NZ, bz, lambda k, w, mats=mats: wall.at[mats, k, :, :, w], at_z, to_z))
        small[1].append(Ring(NZ, bz, lambda k, w, mats=mats: wall.at[mats, k, x, :, w], at_z, to_z))
        large[1].append(Ring(NX, bx, lambda k, w, mats=mats: wall.at[mats, :, k, :, w], at_x, to_x))

    mine[0].wait()
    mine[1].wait()

    def on_core(core, work):
        pl.when(c == core)(functools.partial(work, small[core], large[core]))

    def start_small(small, large):
        for ring in small:
            ring.begin(1)

    on_core(0, start_small)
    on_core(1, start_small)

    named = (ids_t[0:1, :] == iota((NE, F), 0)) | (ids_t[1:2, :] == iota((NE, F), 0))
    before = onehot(iota((F, F), 0) < iota((F, F), 1))
    rank = jnp.where(named, dot(onehot(named), before), -1.0).astype(BF)
    rows = NE * R
    spread = onehot(lax.div(iota((rows, NE), 0), R) == iota((rows, NE), 1))
    rank = dot(spread, rank)
    slot = iota((rows, F), 0)
    pick[...] = onehot(rank == lax.rem(slot, R).astype(F32))
    in_x = rank == (lax.rem(slot, 4) + R).astype(F32)
    for p in range(4):
        pick_x[p] = onehot(in_x & (lax.div(lax.rem(slot, R), 4) == p))

    def small_to_large(small, large):
        for step in range(1, small[0].last):
            for ring in small:
                ring.relay(step)
        for near, wide in zip(small, large):
            near.wait(near.last)
            if wide is not large[-1]:
                wide.begin(1)


    right, left, far = at_y(1), at_y(-1), at_y(2)

    def of_sib(d):
        return d + (1 - 2 * c)

    sent = []

    class Chunk:
        def __init__(self, base, ref, depth):
            self.base, self.ref, self.depth = base, ref, depth

        def copy(self, kind, d, to):
            first = kind in (3, 7)
            rows = pl.ds(0 if first or kind not in (4, 8) else self.depth // 2, self.depth // 2 if kind in (3, 4, 7, 8) else self.depth)
            ref = self.ref.at[d, rows]
            i = self.base + kind
            return remote(ref, ref, w_s.at[i], w_r.at[i], (to, ex))

        def send(self, kind, d, to):
            copy = self.copy(kind, d, to)
            copy.start()
            sent.append(copy)

        def wait(self, kind, d):
            self.copy(kind, d, sib).wait_recv()

        def own(self):
            self.send(0, dp, right)
            self.send(1, dp, left)
            self.send(2, dp, sib)

        def relay(self):
            self.wait(0, left)
            self.send(3, left, right)
            self.send(5, left, sib)
            self.wait(1, right)
            self.send(4, right, left)
            self.send(6, right, sib)

        def relay_far(self):
            self.wait(3, far)
            self.send(7, far, sib)
            self.wait(4, far)
            self.send(8, far, sib)

        def from_sib(self):
            self.wait(2, sib)
            self.wait(5, of_sib(left))
            self.wait(6, of_sib(right))

        def far_from_sib(self):
            self.wait(7, of_sib(far))
            self.wait(8, of_sib(far))

    chunk_in = Chunk(0, win_all, D)
    chunk_out = [Chunk(9, wout_a, H), Chunk(18, wout_b.at[0], H), Chunk(27, wout_b.at[1], H)]
    for copy in mine[2:]:
        copy.wait()
    chunk_in.own()
    on_core(0, small_to_large)
    on_core(1, small_to_large)

    def most(small, large):
        steps = large[0].last
        for step in range(1, min(3, steps)):
            for ring in large[:3]:
                ring.relay(step)
            if step == 1:
                large[3].begin(1)
            else:
                large[3].relay(step - 1)

    on_core(0, most)
    on_core(1, most)

    swap.wait_recv()
    speaker = lax.div(y, NY // 2)
    meeting = lax.rem(dp, NY) * NE + ex
    here = (iota((2, MEETINGS), 0) == speaker) & (iota((2, MEETINGS), 1) == meeting)
    source = jnp.sum(jnp.where(here, order[...], 0).astype(F32), axis=(0, 1), keepdims=True)
    stay = source == speaker.astype(F32)
    stream = jnp.where(stay, frames[...].astype(F32), pbuf[...].astype(F32))
    strm[...] = stream.astype(BF)
    normed[c] = layer_norm(stream, gains[0:1, :]).astype(BF)
    share = remote(normed.at[c], normed.at[c], m_s.at[1], m_r.at[1], (sib, ex))
    share.start()

    def rest(small, large):
        for step in range(3, large[0].last):
            for ring in large[:3]:
                ring.relay(step)
            large[3].relay(step - 1)

    def come(m, small, large):
        large[m].wait(large[m].last)

    def output(steps, small, large):
        step = steps[0] if large[3].last == NZ // 2 else steps[1]
        large[3].relay(step)

    def on_both(work):
        on_core(0, work)
        on_core(1, work)

    on_both(rest)
    remote(
        normed.at[1 - c], normed.at[1 - c], m_s.at[1], m_r.at[1], (sib, ex)
    ).wait_recv()
    chunk_out[0].own()

    for m in range(3):
        on_both(functools.partial(come, m))
        w = wall[m].reshape(D, H)
        for s in range(2):
            proj[m, s] = dot(normed[s], w).astype(BF)
        if m == 1:
            on_both(functools.partial(output, (3, 1)))

    lane = iota((F, 128), 1)

    def attend(s, store):
        @pl.loop(0, H // 128)
        def _(h):
            cols = pl.ds(pl.multiple_of(h * 128, 128), 128)
            q = proj[0, s, :, cols] * jnp.asarray(HEAD_DIM**-0.5, BF)
            k = proj[1, s, :, cols]
            v = proj[2, s, :, cols]
            zero = jnp.zeros_like(q)
            for_both = jnp.concatenate(
                [jnp.where(lane < HEAD_DIM, q, zero), jnp.where(lane < HEAD_DIM, zero, q)], axis=0
            )
            scores = lax.dot_general(
                for_both, k, (((1,), (1,)), ((), ())), preferred_element_type=F32
            )
            scores = jnp.exp(scores - jnp.max(scores, axis=-1, keepdims=True))
            probs = (scores / jnp.sum(scores, axis=-1, keepdims=True)).astype(BF)
            both = dot(probs, v)
            store(cols, jnp.where(lane < HEAD_DIM, both[:F], both[F:]).astype(BF))

    def store_other(cols, value):
        ctxs[:, cols] = value

    def store_own(cols, value):
        ctxh[c, :, cols] = value

    attend(1 - c, store_other)
    on_both(functools.partial(output, (4, 2)))
    give_wo = remote(wall.at[3], wo_sib, m_s.at[2], m_r.at[2], (sib, ex))
    give_wo.start()
    give_ctx = remote(ctxs, ctxh.at[c], m_s.at[3], m_r.at[3], (sib, ex))
    give_ctx.start()
    attend(c, store_own)
    remote(wo_sib, wo_sib, m_s.at[2], m_r.at[2], (sib, ex)).wait_recv()
    remote(
        ctxh.at[1 - c], ctxh.at[1 - c], m_s.at[3], m_r.at[3], (sib, ex)
    ).wait_recv()

    def project(w):
        return dot(ctxh[0], w[:H]) + dot(ctxh[1], w[H:])

    other = pl.ds(pl.multiple_of((1 - c) * H, 128), H)
    mixed[:, half] = (strm[:, half].astype(F32) + project(wall[3].reshape(D, H))).astype(BF)
    mixed[:, other] = (strm[:, other].astype(F32) + project(wo_sib[...].reshape(D, H))).astype(BF)
    chunk_in.relay()
    normed2 = layer_norm(mixed[...].astype(F32), gains[1:2, :]).astype(BF)

    tx[:, :, 0:D] = dot(pick[...], normed2).astype(BF).reshape(NE, R, D)
    packed = dot(pick_x[0], normed2[:, 0:X])
    for p in range(1, 4):
        packed += dot(pick_x[p], normed2[:, p * X : (p + 1) * X])
    tx[:, :, D : D + X] = packed.astype(BF).reshape(NE, R, X)

    def in_z(k):
        i = lax.div(k, NX)
        j, odd = lax.div(i, 2), lax.rem(i, 2)
        return (1 - odd) * lax.rem(NZ // 2 - j, NZ // 2) + odd * (NZ // 2 + j)

    def away(k):
        return lax.rem(z + in_z(k), NZ) * NX + lax.rem(x + lax.rem(k, NX), NX)

    def back(k):
        return lax.rem(z + NZ - in_z(k), NZ) * NX + lax.rem(x + NX - lax.rem(k, NX), NX)

    def send_out(k):
        to = away(k)
        return remote(tx.at[to], rx.at[k], t_s.at[0], t_r.at[lax.div(k, NE // 2)], (dp, to))

    ry, fx = (ry0, ry1, ry2), (fx0, fx1, fx2)

    def give_back(k, q):
        to = back(k)
        return remote(ry[q].at[k], fx[q].at[ex], f_s.at[q], f_r.at[q], (dp, to))

    def all_of(ref, send, recv):
        return remote(ref, ref, send, recv, (sib, ex))

    pl.semaphore_wait(line, NX - 1)

    @pl.loop(1, NE)
    def _(k):
        send_out(k).start()

    rx[0] = tx[ex]

    r0 = router[...].astype(BF)
    r1 = (router[...] - r0.astype(F32)).astype(BF)
    r2 = (router[...] - r0.astype(F32) - r1.astype(F32)).astype(BF)

    def along(b):
        return lax.dot_general(normed2, b, (((1,), (1,)), ((), ())), preferred_element_type=F32)

    logits = along(r0) + (along(r1) + along(r2))
    expert = iota((F, NE), 1)
    chosen = jnp.concatenate([ids_t[...], jnp.zeros((6, F), jnp.int32)], axis=0).astype(F32).T
    chosen = chosen.astype(jnp.int32)
    first, second = chosen[:, 0:1] == expert, chosen[:, 1:2] == expert
    zero = jnp.zeros_like(logits)
    ahead = jnp.sum(jnp.where(first, logits, zero), axis=1, keepdims=True) - jnp.sum(
        jnp.where(second, logits, zero), axis=1, keepdims=True
    )
    gate = 1.0 / (1.0 + jnp.exp(-ahead))
    gates = jnp.where(first, gate, jnp.where(second, 1.0 - gate, zero))
    either = onehot(first | second)
    earlier = onehot(iota((F, F), 1) < iota((F, F), 0))
    rank_f = jnp.where(first | second, dot(earlier, either), -1.0).astype(BF)
    spread_f = onehot(lax.div(iota((NE, rows), 1), R) == iota((NE, rows), 0))
    rank_f = dot(rank_f, spread_f)
    gates_hi = gates.astype(BF)
    gates_lo = (gates - gates_hi.astype(F32)).astype(BF)
    gates_hi, gates_lo = dot(gates_hi, spread_f), dot(gates_lo, spread_f)
    slot_f = iota((F, rows), 1)

    in_place = rank_f == lax.rem(slot_f, R).astype(F32)
    in_tail = rank_f == (lax.rem(slot_f, 4) + R).astype(F32)

    def on(mask, values):
        return jnp.where(mask, values, 0.0).astype(BF)

    quarter = lax.div(lax.rem(slot_f, R), 4)
    weigh[0] = on(in_place, gates_hi)
    weigh[1] = on(in_place, gates_lo)
    for p in range(4):
        here = in_tail & (quarter == p)
        weigh[2 + 2 * p] = on(here, gates_hi)
        weigh[3 + 2 * p] = on(here, gates_lo)


    peers = NE // 2
    whole, more = peers * R, peers * 4
    group = whole + more

    def unpack(p):
        i, j = iota((more, whole), 1), iota((more, whole), 0)
        return onehot(
            (lax.div(i, R) == lax.div(j, 4)) & (lax.rem(i, R) == 4 * p + lax.rem(j, 4))
        )

    def take(g):
        first = max(1, g * peers)
        all_of(rx.at[pl.ds(first, (g + 1) * peers - first)], t_s.at[0], t_r.at[g]).wait_recv()
        mine = slice(g * peers, (g + 1) * peers)
        start = g * group
        xr[start : start + whole] = rx[mine, :, 0:D].reshape(whole, D)
        extra = rx[mine, :, D : D + X].reshape(whole, X)
        for p in range(4):
            xr[start + whole : start + group, p * X : (p + 1) * X] = dot(unpack(p), extra).astype(BF)

    def hide(g, d):
        rows = slice(g * group, (g + 1) * group)
        v = dot(xr[rows], win_all[d])
        hidden[rows, pl.ds(pl.multiple_of(d * H, 128), H)] = (0.5 * v * (1.0 + jnp.tanh(0.5 * v))).astype(BF)

    def answer(g, q):
        rows = slice(g * group, (g + 1) * group)
        mine = slice(g * peers, (g + 1) * peers)
        wide = H if q == 0 else Q
        w = wout_a[...] if q == 0 else wout_b[q - 1]
        acc[:, 0:wide] = dot(hidden[rows], w.reshape(2 * NY * H, wide)).astype(BF)
        ry[q][mine, :, 0:wide] = acc[0:whole, 0:wide].reshape(peers, R, wide)
        start = Q if q == 2 else 0
        tail_y[g, :, start : start + wide] = acc[whole:group, 0:wide]
        if q != 1:
            packed = None
            for p in range(4):
                piece = lax.dot_general(
                    unpack(p),
                    tail_y[g, :, p * 128 : (p + 1) * 128],
                    (((0,), (0,)), ((), ())),
                    preferred_element_type=F32,
                )
                packed = piece if packed is None else packed + piece
            ry[q][mine, :, wide : wide + 128] = packed.astype(BF).reshape(peers, R, 128)

        @pl.loop(max(1, g * peers), (g + 1) * peers)
        def _(k):
            give_back(k, q).start()

        if g == 0:
            fx[q][ex] = ry[q][0]

    def finish_far(chunk):
        chunk.relay_far()
        chunk.from_sib()
        chunk.far_from_sib()

    def sent_all():
        for copy in sent + [swap, share, give_wo, give_ctx]:
            copy.wait_send()

        def finish(small, large):
            for ring in small + large:
                ring.finish()

        on_both(finish)
        all_of(tx.at[pl.ds(0, NE - 1)], t_s.at[0], t_r.at[0]).wait_send()

    chunk_out[0].relay()
    chunk_out[1].own()
    chunk_out[2].own()
    take(0)
    hide(0, dp)
    chunk_in.from_sib()
    for d in (sib, left, right, of_sib(left), of_sib(right)):
        hide(0, d)
    chunk_in.relay_far()
    hide(0, far)
    chunk_in.far_from_sib()
    hide(0, of_sib(far))
    finish_far(chunk_out[0])
    answer(0, 0)
    take(1)
    chunk_out[1].relay()
    for d in (dp, sib, left, right, of_sib(left), of_sib(right), far, of_sib(far)):
        hide(1, d)
    chunk_out[2].relay()
    answer(1, 0)
    finish_far(chunk_out[1])
    answer(0, 1)
    answer(1, 1)
    finish_far(chunk_out[2])
    answer(0, 2)
    answer(1, 2)
    sent_all()

    def wait_for(q):
        all_of(fx[q].at[pl.ds(0, NE - 1)], f_s.at[q], f_r.at[q]).wait_recv()
        wide = H if q == 0 else Q
        body = fx[q][:, :, 0:wide].reshape(rows, wide)
        return dot(weigh[0], body) + dot(weigh[1], body)

    def combine(start, main, last):
        for p in range(4):
            cols = slice(start + p * 128, start + (p + 1) * 128)
            i = 0 if len(main) == 1 else p // 2
            at = (p if len(main) == 1 else p % 2) * 128
            out[:, cols] = (
                mixed[:, cols].astype(F32)
                + main[i][:, at : at + 128]
                + (dot(weigh[2 + 2 * p], last) + dot(weigh[3 + 2 * p], last))
            ).astype(BF)

    main = [wait_for(0)]
    combine(0, main, fx0[:, :, H : H + 128].reshape(rows, 128))
    main = [wait_for(1), wait_for(2)]
    combine(H, main, fx2[:, :, Q : Q + 128].reshape(rows, 128))
    for q in range(3):
        all_of(ry[q].at[pl.ds(0, NE - 1)], f_s.at[q], f_r.at[q]).wait_send()


def body(
    frames_in, pit_order, expert_ids, norm_gains, attn_qkv, attn_out, router, expert_in, expert_out
):
    vmem = pl.BlockSpec(memory_space=pltpu.VMEM)
    hbm = pl.BlockSpec(memory_space=pl.ANY)
    dma = pltpu.SemaphoreType.DMA
    rows = NE * R
    out = pl.pallas_call(
        kernel,
        out_shape=jax.ShapeDtypeStruct((F, D), BF),
        in_specs=[vmem] * 5 + [hbm] * 4,
        out_specs=vmem,
        scratch_shapes=[
            pltpu.VMEM((F, D), BF),
            pltpu.VMEM((F, D), BF),
            pltpu.VMEM((2, F, D), BF),
            pltpu.VMEM((4, NZ, NX, D // NE, H), BF),
            pltpu.VMEM((NZ, NX, D // NE, H), BF),
            pltpu.VMEM((3, 2, F, H), BF),
            pltpu.VMEM((2, F, H), BF),
            pltpu.VMEM((F, H), BF),
            pltpu.VMEM((F, D), BF),
            pltpu.VMEM((NE, R, D + X), BF),
            pltpu.VMEM((NE, R, D + X), BF),
            pltpu.VMEM((NE, R, H + 128), BF),
            pltpu.VMEM((NE, R, Q), BF),
            pltpu.VMEM((NE, R, Q + 128), BF),
            pltpu.VMEM((NE, R, H + 128), BF),
            pltpu.VMEM((NE, R, Q), BF),
            pltpu.VMEM((NE, R, Q + 128), BF),
            pltpu.VMEM((NE * CAP, D), BF),
            pltpu.VMEM((NE * CAP, 2 * NY * H), BF),
            pltpu.VMEM((NE // 2 * CAP, H), BF),
            pltpu.VMEM((2, NE // 2 * 4, H), BF),
            pltpu.VMEM((2 * NY, D, H), BF),
            pltpu.VMEM((2 * NY, H, H), BF),
            pltpu.VMEM((2, 2 * NY, H, Q), BF),
            pltpu.VMEM((10, F, rows), BF),
            pltpu.VMEM((rows, F), BF),
            pltpu.VMEM((4, rows, F), BF),
            dma((48,)),
            dma((48,)),
            dma((36,)),
            dma((36,)),
            dma((4,)),
            dma((4,)),
            dma((1,)),
            dma((2,)),
            dma((3,)),
            dma((3,)),
            dma((6,)),
            pltpu.SemaphoreType.REGULAR,
        ],
        compiler_params=pltpu.CompilerParams(
            collective_id=0, has_side_effects=True, vmem_limit_bytes=60 * 2**20
        ),
        cost_estimate=pl.CostEstimate(
            flops=14 * 10**9, bytes_accessed=8 * 2**20, transcendentals=4 * 10**6
        ),
    )(
        pit_order.T,
        expert_ids[0].T,
        norm_gains,
        router.T,
        frames_in[0],
        attn_qkv,
        attn_out,
        expert_in[0],
        expert_out[0],
    )
    return out[None]


def solution(mesh):
    return jax.shard_map(
        body,
        mesh=mesh,
        in_specs=(
            P(("dp", "expert"), None, None),
            P(),
            P(("dp", "expert"), None, None),
            P(),
            P(None, "expert", None),
            P("expert", None),
            P(),
            P("expert", None, "dp"),
            P("expert", "dp", None),
        ),
        out_specs=P(("dp", "expert"), None, None),
        check_vma=False,
    )
```
